256 devices in a mesh: dp: 256 (over y, z, x, core).
Axes of the slice: x: 4, y: 4, z: 8, core: 2. Of those that a mesh axis runs over, the one named last changes fastest.
Arguments:
- images: float32 [131072, 1152], P('dp'), may hold values from -1.0298836 to 1.0298836
- texts: float32 [131072, 1152], P('dp'), may hold values from -1.0298836 to 1.0298836
- logit_scale: float32 [1], replicated, may hold values from 2 to 6
- logit_bias: float32 [1], replicated, may hold values from -4 to -1
Outputs:
- image_grad: float32 [131072, 1152], P('dp')
- text_grad: float32 [131072, 1152], P('dp')
The draws below stay inside these ranges and needn't reach their ends.
All inputs are finite; a program needn't handle non-finite values.
Results may differ from the reference program's by a relative error of at most 0.000088.
Values sent between devices are 32-bit elements; how exact they have to be, the bound alone decides.
No kernel may reach another device: no remote copies, remote signals or barrier semaphores. Data moves between devices by JAX's collectives and lax.ppermute only.
A program may use at most 64 MiB of HBM per device.

```python
import jax
import jax.numpy as jnp
from jax import lax

D = 1152
B_DEV = 512
TOKENS = 131072
N_DP = 256


def steps_of(own_key, extent, pieces, low, largest):
    loudness = 1.0
    for axis_at, blocks in pieces:
        heights = jax.random.uniform(jax.random.fold_in(jax.random.fold_in(own_key, 6), axis_at), (blocks,), jnp.float32, low / len(pieces), largest / len(pieces))
        loudness = loudness * jnp.repeat(jnp.exp(heights), extent[axis_at] // blocks).reshape((-1,) + (1,) * (len(extent) - 1 - axis_at))
    return loudness


def centred(rng, extent, scale, reach, shards=(), held_as=jnp.bfloat16):
    drawn = scale * jax.random.normal(rng, extent, jnp.float32)
    if shards:
        drawn = drawn * steps_of(rng, extent, shards, -0.22, 0.18)
    return jnp.clip(drawn, -reach, reach).astype(held_as)


def setup_inputs(seed: int = 0) -> dict:
    seeds = jax.random.split(jax.random.key(seed), 5)
    return {
        "images": centred(seeds[0], (TOKENS, D), (D ** -0.25), 1.0298836, ((0, 256),), jnp.float32),
        "texts": centred(seeds[1], (TOKENS, D), (D ** -0.25), 1.0298836, ((0, 256),), jnp.float32),
        "logit_scale": jnp.clip(jax.random.uniform(seeds[2], (1,), jnp.float32, 2.0, 6.0), 2.0, 6.0),
        "logit_bias": jnp.clip(jax.random.uniform(seeds[3], (1,), jnp.float32, -4.0, -1.0), -4.0, -1.0),
    }


def block_terms(images, texts, scale, bias, labels):
    logits = scale * jnp.dot(images, texts.T, precision=lax.Precision.HIGHEST, preferred_element_type=jnp.float32) + bias
    coef = -labels * scale * jax.nn.sigmoid(-labels * logits)
    grad_images = jnp.dot(coef, texts, precision=lax.Precision.HIGHEST, preferred_element_type=jnp.float32)
    grad_texts = lax.dot_general(coef, images, (((0,), (0,)), ((), ())), precision=lax.Precision.HIGHEST, preferred_element_type=jnp.float32)
    return grad_images, grad_texts


def reference(images, texts, logit_scale, logit_bias):
    scale = logit_scale[0]
    bias = logit_bias[0]
    image_blocks = images.reshape(N_DP, B_DEV, D)
    text_blocks = texts.reshape(N_DP, B_DEV, D)
    positive = 2.0 * jnp.eye(B_DEV, dtype=jnp.float32) - 1.0
    negative = -jnp.ones((B_DEV, B_DEV), jnp.float32)

    def per_block(items):
        image_rows, own_texts, near_texts, far_texts = items
        grad_own, text_own = block_terms(image_rows, own_texts, scale, bias, positive)
        grad_near, text_near = block_terms(image_rows, near_texts, scale, bias, negative)
        grad_far, text_far = block_terms(image_rows, far_texts, scale, bias, negative)
        return grad_own + grad_near + grad_far, text_own, text_near, text_far

    image_grad, text_own, text_near, text_far = lax.map(per_block, (image_blocks, text_blocks, jnp.roll(text_blocks, 1, 0), jnp.roll(text_blocks, 2, 0)))
    text_grad = text_own + jnp.roll(text_near, -1, 0) + jnp.roll(text_far, -2, 0)
    return image_grad.reshape(TOKENS, D), text_grad.reshape(TOKENS, D)
```

```python
import functools

import jax
import jax.numpy as jnp
from jax import lax
from jax.experimental import pallas as pl
from jax.experimental.pallas import tpu as pltpu
from jax.sharding import PartitionSpec as P

F32 = jnp.float32
BF16 = jnp.bfloat16
ANY = pl.BlockSpec(memory_space=pl.ANY)
SMEM = pl.BlockSpec(memory_space=pltpu.SMEM)
VMEM_LIMIT = 40 * 1024 * 1024

FIRST = (128, 384)
SECOND = (384, 128)


def halves(x):
    high = x.astype(BF16)
    return high, (x - high.astype(F32)).astype(BF16)


def dot3(xs, ys, dims):
    def one(x, y):
        return lax.dot_general(x, y, (dims, ((), ())), preferred_element_type=F32)

    return one(xs[0], ys[0]) + (one(xs[0], ys[1]) + one(xs[1], ys[0]))


def sigmoid(x):
    return 1.0 / (1.0 + jnp.exp(-x))


def offsets(rows):
    starts, at = [], 0
    for r in rows:
        starts.append(at)
        at += r
    return starts


def is_even():
    return lax.rem(lax.axis_index("dp"), 2) == 0


def pick_kernel(parts, images, texts, *refs):
    outs, sems = refs[:-1], refs[-1]

    def copies(even):
        for i, (own, start, rows) in enumerate(parts):
            source = images if own == even else texts
            yield pltpu.make_async_copy(source.at[pl.ds(start, rows)], outs[i], sems.at[i])

    def run(even):
        started = list(copies(even))
        for copy in started:
            copy.start()
        for copy in started:
            copy.wait()

    even = is_even()
    pl.when(even)(lambda: run(True))
    pl.when(jnp.logical_not(even))(lambda: run(False))


def pick(images, texts, parts):
    width = images.shape[1]
    return pl.pallas_call(
        functools.partial(pick_kernel, parts),
        out_shape=[jax.ShapeDtypeStruct((rows, width), F32) for _, _, rows in parts],
        in_specs=[ANY, ANY],
        out_specs=[ANY] * len(parts),
        scratch_shapes=[pltpu.SemaphoreType.DMA((len(parts),))],
        cost_estimate=pl.CostEstimate(
            flops=0, bytes_accessed=sum(8 * rows * width for _, _, rows in parts), transcendentals=0
        ),
        name="pick",
    )(images, texts)


def own_kernel(na, nb, tile, scale_ref, bias_ref, *refs):
    a_refs, b_refs = refs[:na], refs[na : na + nb]
    ga, gb, ah, al, bh, bl = refs[na + nb :]
    for pieces, high, low in ((a_refs, ah, al), (b_refs, bh, bl)):
        for start, piece in zip(offsets([p.shape[0] for p in pieces]), pieces):
            h, l = halves(piece[...])
            rows = pl.ds(start, piece.shape[0])
            high[rows, :] = h
            low[rows, :] = l
    scale, bias = scale_ref[0], bias_ref[0]
    total = ah.shape[0]
    ys = (bh[...], bl[...])
    for t in range(total // tile):
        rows = pl.ds(t * tile, tile)
        xs = (ah[rows, :], al[rows, :])
        logits = scale * dot3(xs, ys, ((1,), (1,))) + bias
        shape = logits.shape
        diagonal = lax.broadcasted_iota(jnp.int32, shape, 0) + t * tile == (
            lax.broadcasted_iota(jnp.int32, shape, 1)
        )
        sign = jnp.where(diagonal, -1.0, 1.0).astype(F32)
        coef = halves(sign * scale * sigmoid(sign * logits))
        ga[rows, :] = dot3(coef, ys, ((1,), (0,)))
        side = dot3(coef, xs, ((0,), (0,)))
        gb[...] = side if t == 0 else gb[...] + side


def own(a, b, scale, bias):
    rows = sum(x.shape[0] for x in a)
    width = a[0].shape[1]
    wide = jax.ShapeDtypeStruct((rows, width), F32)
    thin = jax.ShapeDtypeStruct((rows, width), BF16)
    return pl.pallas_call(
        functools.partial(own_kernel, len(a), len(b), 256),
        out_shape=[wide, wide, thin, thin, thin, thin],
        in_specs=[SMEM, SMEM] + [pl.BlockSpec(memory_space=pltpu.VMEM)] * (len(a) + len(b)),
        out_specs=[pl.BlockSpec(memory_space=pltpu.VMEM)] * 6,
        compiler_params=pltpu.CompilerParams(vmem_limit_bytes=VMEM_LIMIT),
        cost_estimate=pl.CostEstimate(
            flops=18 * rows * rows * width, bytes_accessed=24 * rows * width, transcendentals=rows * rows
        ),
        name="own_pair",
    )(scale, bias, *a, *b)


def pair_kernel(ny, tile, steps, place, scale_ref, bias_ref, *refs):
    y_refs, (xh, xl, acc) = refs[:ny], refs[ny : ny + 3]
    refs = refs[ny + 3 :]
    if place is None:
        out, yh, yl = refs
    else:
        images_out, texts_out, yh, yl, result, sems = refs[-6:]
    step = pl.program_id(0)

    @pl.when(step == 0)
    def _():
        for start, piece in zip(offsets([p.shape[0] for p in y_refs]), y_refs):
            h, l = halves(piece[...])
            rows = pl.ds(start, piece.shape[0])
            yh[rows, :] = h
            yl[rows, :] = l

    scale, bias = scale_ref[0], bias_ref[0]
    ys = (yh[...], yl[...])
    logits = scale * dot3((xh[...], xl[...]), ys, ((1,), (1,))) + bias
    coef = halves(scale * sigmoid(logits))
    value = acc[...] + dot3(coef, ys, ((1,), (0,)))
    if place is None:
        out[...] = value
        return
    rows = pl.ds(pl.multiple_of(step * tile, tile), tile)
    result[rows, :] = value
    to_images = is_even() if place else jnp.logical_not(is_even())

    def copy(target, at):
        span = pl.ds(pl.multiple_of(at * tile, tile), tile)
        return pltpu.make_async_copy(result.at[span], target.at[span], sems.at[at])

    pl.when(to_images)(lambda: copy(images_out, step).start())
    pl.when(jnp.logical_not(to_images))(lambda: copy(texts_out, step).start())

    @pl.when(step == steps - 1)
    def _():
        def finish(target):
            for at in range(steps):
                copy(target, at).wait()

        pl.when(to_images)(lambda: finish(images_out))
        pl.when(jnp.logical_not(to_images))(lambda: finish(texts_out))


def pair(x, ys, acc, scale, bias, tile=256, place=None, into=()):
    xh, xl = x
    rows, width = xh.shape
    depth = sum(y.shape[0] for y in ys)
    steps = rows // tile
    wide = jax.ShapeDtypeStruct((rows, width), F32)
    tiled = pl.BlockSpec((tile, width), lambda i: (i, 0))
    whole = [
        pl.BlockSpec(y.shape, lambda i: (0, 0), pipeline_mode=pl.Buffered(1)) for y in ys
    ]
    scratch = [pltpu.VMEM((depth, width), BF16)] * 2
    aliases = {}
    if place is None:
        out_shape, out_specs = wide, tiled
    else:
        out_shape, out_specs = [wide, wide], [ANY, ANY]
        scratch = scratch + [pltpu.VMEM((rows, width), F32), pltpu.SemaphoreType.DMA((steps,))]
        first = 2 + len(ys) + 3
        aliases = {first + i: i for i in range(len(into))}
    return pl.pallas_call(
        functools.partial(pair_kernel, len(ys), tile, steps, place),
        grid=(steps,),
        out_shape=out_shape,
        in_specs=[SMEM, SMEM] + whole + [tiled] * 3 + [ANY] * len(into),
        out_specs=out_specs,
        scratch_shapes=scratch,
        input_output_aliases=aliases,
        compiler_params=pltpu.CompilerParams(
            vmem_limit_bytes=VMEM_LIMIT, dimension_semantics=("arbitrary",)
        ),
        cost_estimate=pl.CostEstimate(
            flops=12 * rows * depth * width,
            bytes_accessed=4 * width * (3 * rows + depth),
            transcendentals=rows * depth,
        ),
        name="pair",
    )(scale, bias, *ys, xh, xl, acc, *into)


def body(images, texts, scale, bias):
    peers = lax.axis_size("dp")

    def over_link(x):
        return lax.ppermute(
            x, "dp", [(i, (i + 1) % peers if i % 2 else (i - 1) % peers) for i in range(peers)]
        )

    def on_chip(x):
        return lax.ppermute(x, "dp", [(i, i ^ 1) for i in range(peers)])

    starts = offsets(FIRST)
    head = pick(images, texts, [(True, starts[0], FIRST[0])])
    rest = pick(
        images,
        texts,
        [(True, s, r) for s, r in zip(starts[1:], FIRST[1:])]
        + [(False, s, r) for s, r in zip(offsets(SECOND), SECOND)],
    )
    a = head + rest[: len(FIRST) - 1]
    b = rest[len(FIRST) - 1 :]
    a1 = [over_link(x) for x in a]
    b1 = [on_chip(x) for x in b]
    a2 = [over_link(x) for x in b1]
    b2 = [on_chip(x) for x in a1]

    ga, gb, ah, al, bh, bl = own(a, b, scale, bias)
    gb = pair((bh, bl), b1, gb, scale, bias)
    ga = pair((ah, al), a1, ga, scale, bias)
    outs = pair((bh, bl), b2, gb, scale, bias, place=False)
    ga = pair((ah, al), a2[:-1], ga, scale, bias)
    outs = pair((ah, al), a2[-1:], ga, scale, bias, tile=128, place=True, into=outs)
    return tuple(outs)


def solution(mesh):
    in_specs = (P("dp", None), P("dp", None), P(), P())
    out_specs = (P("dp", None), P("dp", None))
    return jax.shard_map(body, mesh=mesh, in_specs=in_specs, out_specs=out_specs, check_vma=False)
```

```python
import functools

import jax
import jax.numpy as jnp
from jax import lax
from jax.experimental import pallas as pl
from jax.experimental.pallas import tpu as pltpu
from jax.sharding import PartitionSpec as P

F32 = jnp.float32
BF16 = jnp.bfloat16
ANY = pl.BlockSpec(memory_space=pl.ANY)
VMEM = pl.BlockSpec(memory_space=pltpu.VMEM)
SMEM = pl.BlockSpec(memory_space=pltpu.SMEM)
VMEM_LIMIT = 20 * 1024 * 1024

HINT = 10

SECOND = (384, 128)
FIRST = (128, 192, 192)
TAIL_TILE = 256


def halves(x):
    high = x.astype(BF16)
    return high, (x - high.astype(F32)).astype(BF16)


def dot3(xs, ys, dims):
    def one(x, y):
        return lax.dot_general(x, y, (dims, ((), ())), preferred_element_type=F32)

    return one(xs[0], ys[0]) + (one(xs[0], ys[1]) + one(xs[1], ys[0]))


def sigmoid(x):
    return 1.0 / (1.0 + jnp.exp(-x))


def offsets(rows):
    starts, at = [], 0
    for r in rows:
        starts.append(at)
        at += r
    return starts


def in_vmem(x):
    return pltpu.with_memory_space_constraint(x, pltpu.VMEM)


def is_even():
    return lax.rem(lax.axis_index("dp"), 2) == 0


def by_side(to_images, run):
    pl.when(to_images)(lambda: run(0))
    pl.when(jnp.logical_not(to_images))(lambda: run(1))


def own_kernel(tile, scale_ref, bias_ref, images, texts, gi, gt, ih, il, th, tl):
    rows = ih.shape[0]
    steps = rows // tile
    scale, bias = scale_ref[0], bias_ref[0]
    for t in range(steps):
        span = pl.ds(t * tile, tile)
        th[span, :], tl[span, :] = halves(texts[span, :])
    ys = (th[...], tl[...])
    for t in range(steps):
        span = pl.ds(t * tile, tile)
        xs = halves(images[span, :])
        ih[span, :], il[span, :] = xs
        logits = scale * dot3(xs, ys, ((1,), (1,))) + bias
        shape = logits.shape
        diagonal = lax.broadcasted_iota(jnp.int32, shape, 0) + t * tile == (
            lax.broadcasted_iota(jnp.int32, shape, 1)
        )
        sign = jnp.where(diagonal, -1.0, 1.0).astype(F32)
        coef = halves(sign * scale * sigmoid(sign * logits))
        gi[span, :] = dot3(coef, ys, ((1,), (0,)))
        side = dot3(coef, xs, ((0,), (0,)))
        gt[...] = side if t == 0 else gt[...] + side


def own(images, texts, scale, bias):
    rows, width = images.shape
    tile = 256
    wide = jax.ShapeDtypeStruct((rows, width), F32)
    thin = jax.ShapeDtypeStruct((rows, width), BF16)
    return pl.pallas_call(
        functools.partial(own_kernel, tile),
        out_shape=[wide, wide, thin, thin, thin, thin],
        in_specs=[SMEM, SMEM, VMEM, VMEM],
        out_specs=[VMEM] * 6,
        compiler_params=pltpu.CompilerParams(vmem_limit_bytes=VMEM_LIMIT),
        cost_estimate=pl.CostEstimate(
            flops=HINT * 18 * rows * rows * width, bytes_accessed=24 * rows * width, transcendentals=rows * rows
        ),
        name="own_pair",
    )(scale, bias, in_vmem(images), in_vmem(texts))


def pair_kernel(ny, tile, linked, final, scale_ref, bias_ref, *refs):
    y_refs, (ih, il, th, tl, gi, gt), refs = refs[:ny], refs[ny : ny + 6], refs[ny + 6 :]
    outs = refs[-4:-2] if final else refs[-2:]
    scale, bias = scale_ref[0], bias_ref[0]
    rows = ih.shape[0]
    steps = rows // tile

    def run(side):
        xh, xl, acc = ((ih, il, gi), (th, tl, gt))[side]
        out = outs[side]
        result, sems = refs[-2:] if final else (out, None)
        pieces = [halves(y[...]) for y in y_refs]
        ys = tuple(jnp.concatenate(p, axis=0) if ny > 1 else p[0] for p in zip(*pieces))
        copies = []
        for at in range(steps):
            span = pl.ds(at * tile, tile)
            logits = scale * dot3((xh[span, :], xl[span, :]), ys, ((1,), (1,))) + bias
            coef = halves(scale * sigmoid(logits))
            result[span, :] = acc[span, :] + dot3(coef, ys, ((1,), (0,)))
            if final:
                copies.append(pltpu.make_async_copy(result.at[span], out.at[span], sems.at[at]))
                copies[-1].start()
        for copy in copies:
            copy.wait()

    by_side(is_even() if linked else jnp.logical_not(is_even()), run)


def pair(blocks, ys, grads, scale, bias, linked, tile=256, final=False, into=()):
    rows, width = blocks[0].shape
    depth = sum(y.shape[0] for y in ys)
    wide = jax.ShapeDtypeStruct((rows, width), F32)
    first = 2 + len(ys) + 4
    if final:
        aliases = {first + 2 + i: i for i in range(len(into))}
        scratch = [pltpu.VMEM((rows, width), F32), pltpu.SemaphoreType.DMA((rows // tile,))]
    else:
        aliases = {first: 0, first + 1: 1}
        scratch = []
    return pl.pallas_call(
        functools.partial(pair_kernel, len(ys), tile, linked, final),
        out_shape=[wide, wide],
        in_specs=[SMEM, SMEM] + [VMEM] * (len(ys) + 6) + [ANY] * len(into),
        out_specs=[ANY if final else VMEM] * 2,
        scratch_shapes=scratch,
        input_output_aliases=aliases,
        compiler_params=pltpu.CompilerParams(vmem_limit_bytes=VMEM_LIMIT),
        cost_estimate=pl.CostEstimate(
            flops=12 * rows * depth * width,
            bytes_accessed=4 * width * (3 * rows + depth),
            transcendentals=rows * depth,
        ),
        name="pair",
    )(scale, bias, *map(in_vmem, ys), *map(in_vmem, blocks), *map(in_vmem, grads), *into)


def after(value, *earlier):
    return lax.optimization_barrier((value, earlier))[0]


def body(images, texts, scale, bias):
    peers = lax.axis_size("dp")

    def over_link(x):
        return lax.ppermute(
            x, "dp", [(i, (i + 1) % peers if i % 2 else (i - 1) % peers) for i in range(peers)]
        )

    def on_chip(x):
        return lax.ppermute(x, "dp", [(i, i ^ 1) for i in range(peers)])

    even = is_even()
    a = [jnp.where(even, images[s : s + r], texts[s : s + r]) for s, r in zip(offsets(FIRST), FIRST)]
    b = jnp.where(even, *after((texts, images), a))
    a1 = [over_link(x) for x in a]
    b1 = on_chip(b)
    gi, gt, *blocks = own(*after((images, texts), b), scale, bias)
    b1 = after(b1, gi)
    a2 = [over_link(b1[start : start + r]) for start, r in zip(offsets(SECOND), SECOND)]
    grads = pair(blocks, [b1], (gi, gt), scale, bias, linked=False)
    a1 = after(a1, grads)
    b2 = [on_chip(x) for x in a1]
    grads = pair(blocks, a1, grads, scale, bias, linked=True)
    outs = pair(blocks, b2, grads, scale, bias, linked=False, final=True)
    grads = pair(blocks, after(a2[:1], outs), grads, scale, bias, linked=True)
    outs = pair(
        blocks, after(a2[1:], grads), grads, scale, bias, linked=True, tile=TAIL_TILE, final=True, into=outs
    )
    return tuple(outs)


def solution(mesh):
    in_specs = (P("dp", None), P("dp", None), P(), P())
    out_specs = (P("dp", None), P("dp", None))
    return jax.shard_map(body, mesh=mesh, in_specs=in_specs, out_specs=out_specs, check_vma=False)
```

```python
import functools

import jax
import jax.numpy as jnp
from jax import lax
from jax.experimental import pallas as pl
from jax.experimental.pallas import tpu as pltpu
from jax.sharding import PartitionSpec as P

F32 = jnp.float32
BF16 = jnp.bfloat16
ANY = pl.BlockSpec(memory_space=pl.ANY)
VMEM = pl.BlockSpec(memory_space=pltpu.VMEM)
VMEM_LIMIT = 20 * 1024 * 1024

HINT = 10

SECOND = (384, 128)
RETURN = (256, 256)
TILE = 256
COLUMNS = 384


def halves(x):
    high = x.astype(BF16)
    return high, (x - high.astype(F32)).astype(BF16)


def dot3(xs, ys, dims):
    def one(x, y):
        return lax.dot_general(x, y, (dims, ((), ())), preferred_element_type=F32)

    return one(xs[0], ys[0]) + (one(xs[0], ys[1]) + one(xs[1], ys[0]))


def sigmoid(x):
    return 1.0 / (1.0 + jnp.exp(-x))


def offsets(rows):
    starts, at = [], 0
    for r in rows:
        starts.append(at)
        at += r
    return starts


def spans(total, tile):
    return [pl.ds(start, tile) for start in range(0, total, tile)]


def is_even():
    return lax.rem(lax.axis_index("dp"), 2) == 0


def wide(*shape):
    return jax.ShapeDtypeStruct(shape, F32)


def thin(*shape):
    return jax.ShapeDtypeStruct(shape, BF16)


def call(kernel, name, args, in_specs, out_shape, out_specs, flops, scratch=(), aliases=None):
    return pl.pallas_call(
        kernel,
        out_shape=out_shape,
        in_specs=in_specs,
        out_specs=out_specs,
        scratch_shapes=list(scratch),
        input_output_aliases=aliases or {},
        compiler_params=pltpu.CompilerParams(vmem_limit_bytes=VMEM_LIMIT),
        cost_estimate=pl.CostEstimate(flops=flops, bytes_accessed=4 * 1024 * 1024, transcendentals=512 * 512),
        name=name,
    )(*args)


def joined(parts, axis):
    return jnp.concatenate(parts, axis=axis)


def one_dot(x, y, dims):
    return lax.dot_general(x, y, (dims, ((), ())), preferred_element_type=F32)


def scores(xs, ys):
    (xh, xl), (yh, yl) = xs, ys
    return one_dot(joined([xh, xh, xl], 1), joined([yh, yl, yh], 1), ((1,), (1,)))


def weighted(cs, ys):
    (ch, cl), (yh, yl) = cs, ys
    return one_dot(joined([ch, ch, cl], 1), joined([yh, yl, yh], 0), ((1,), (0,)))


def coefs(xs, ys, params):
    scale, bias = params[0:1, 0:1], params[8:9, 0:1]
    return halves(scale * sigmoid(scale * scores(xs, ys) + bias))


def term(xs, ys, params):
    return weighted(coefs(xs, ys, params), ys)


def link_side():
    return lax.rem(lax.axis_index("dp"), 2)


def to_output(side, source, targets, sem):
    for k in range(2):
        pl.when(side == k)(pltpu.make_async_copy(source, targets[k], sem).start)


def own_kernel(scale_ref, bias_ref, images, texts, grads, high, low, params):
    for k, block in enumerate((images, texts)):
        high[k], low[k] = halves(block[...])
    scale, bias = scale_ref[...], bias_ref[...]
    params[0:8, :] = jnp.broadcast_to(scale, (8, 128))
    params[8:16, :] = jnp.broadcast_to(bias, (8, 128))
    ys = (high[1], low[1])
    for t, span in enumerate(spans(images.shape[0], TILE)):
        xs = (high[0, span, :], low[0, span, :])
        logits = scale * scores(xs, ys) + bias
        shape = logits.shape
        diagonal = lax.broadcasted_iota(jnp.int32, shape, 0) + t * TILE == (
            lax.broadcasted_iota(jnp.int32, shape, 1)
        )
        sign = jnp.where(diagonal, -1.0, 1.0).astype(F32)
        coef = halves(sign * scale * sigmoid(sign * logits))
        grads[0, span, :] = weighted(coef, ys)
        side = dot3(coef, xs, ((0,), (0,)))
        grads[1] = side if t == 0 else grads[1] + side


def own(images, texts, scale, bias):
    rows, width = images.shape
    return call(
        own_kernel,
        "own_pair",
        (scale.reshape(1, 1), bias.reshape(1, 1), images, texts),
        [VMEM] * 4,
        [wide(2, rows, width), thin(2, rows, width), thin(2, rows, width), wide(16, 128)],
        [VMEM] * 4,
        HINT * 18 * rows * rows * width,
    )


def near_kernel(params, y, high, low, grads, grads_out, yh, yl):
    side = 1 - link_side()
    ys = halves(y[...])
    yh[...], yl[...] = ys
    for span in spans(y.shape[0], TILE):
        xs = (high[side, span, :], low[side, span, :])
        grads_out[side, span, :] = grads[side, span, :] + term(xs, ys, params)


def near(params, y, high, low, grads):
    rows, width = y.shape
    return call(
        near_kernel,
        "near_pair",
        (params, y, high, low, grads),
        [VMEM] * 5,
        [wide(2, rows, width)] + [thin(rows, width)] * 2,
        [VMEM] * 3,
        12 * rows * rows * width,
        aliases={4: 0},
    )


def mate_kernel(params, xh, xl, y, *refs):
    outs, (yh, yl) = refs[:-2], refs[-2:]
    ys = halves(y[...])
    yh[...], yl[...] = ys
    for start, out in zip(offsets([out.shape[0] for out in outs]), outs):
        span = pl.ds(start, out.shape[0])
        out[...] = term((xh[span, :], xl[span, :]), ys, params)


def mate(params, xh, xl, y):
    rows, width = xh.shape
    return call(
        mate_kernel,
        "mate_pair",
        (params, xh, xl, y),
        [VMEM] * 4,
        [wide(r, width) for r in RETURN] + [thin(rows, width)] * 2,
        [VMEM] * (len(RETURN) + 2),
        12 * rows * rows * width,
    )


def link_kernel(params, yh, yl, high, low, grads, grads_out):
    side = link_side()
    ys = (yh[...], yl[...])
    for span in spans(yh.shape[0], TILE):
        xs = (high[side, span, :], low[side, span, :])
        grads_out[side, span, :] = grads[side, span, :] + term(xs, ys, params)


def link(params, ys, high, low, grads):
    _, rows, width = grads.shape
    return call(
        link_kernel,
        "link_pair",
        (params, *ys, high, low, grads),
        [VMEM] * 6,
        wide(2, rows, width),
        VMEM,
        12 * rows * rows * width,
        aliases={5: 0},
    )


def far_kernel(nr, params, y, *refs):
    terms, (high, low, grads, grads_out, images_out, texts_out, result, sems) = refs[:nr], refs[nr:]
    side = link_side()
    starts = offsets([piece.shape[0] for piece in terms])
    for i, (start, piece) in enumerate(zip(starts, terms)):
        span = pl.ds(start, piece.shape[0])
        result[span, :] = grads[1 - side, span, :] + piece[...]
        to_output(1 - side, result.at[span], (images_out.at[span], texts_out.at[span]), sems.at[i])
    ys = halves(y[...])
    for span in spans(grads.shape[1], TILE):
        xs = (high[side, span, :], low[side, span, :])
        grads_out[side, span, :] = grads[side, span, :] + term(xs, ys, params)
    for i, (start, piece) in enumerate(zip(starts, terms)):
        span = pl.ds(start, piece.shape[0])
        pltpu.make_async_copy(result.at[span], images_out.at[span], sems.at[i]).wait()


def far(params, y, terms, high, low, grads):
    _, rows, width = grads.shape
    first = 2 + len(terms) + 2
    return call(
        functools.partial(far_kernel, len(terms)),
        "far_pair",
        (params, y, *terms, high, low, grads),
        [VMEM] * (first + 1),
        [wide(2, rows, width)] + [wide(rows, width)] * 2,
        [VMEM, ANY, ANY],
        12 * rows * y.shape[0] * width,
        [pltpu.VMEM((rows, width), F32), pltpu.SemaphoreType.DMA((len(terms),))],
        {first: 0},
    )


def last_kernel(params, y, high, low, grads, images_in, texts_in, images_out, texts_out, result, sems):
    side = link_side()
    yh, yl = halves(y[...])
    depth, width = y.shape
    xh, xl = high[side], low[side]
    both = one_dot(xh, joined([yh, yl], 0), ((1,), (1,)))
    total = both[:, :depth] + both[:, depth:] + one_dot(xl, yh, ((1,), (1,)))
    scale, bias = params[0:1, 0:1], params[8:9, 0:1]
    ch, cl = halves(scale * sigmoid(scale * total + bias))
    cs = joined([ch, cl, ch], 1)
    for i, start in enumerate(range(0, width, COLUMNS)):
        span = pl.ds(start, COLUMNS)
        yc = joined([yh[:, start : start + COLUMNS]] * 2 + [yl[:, start : start + COLUMNS]], 0)
        result[:, span] = grads[side, :, span] + one_dot(cs, yc, ((1,), (0,)))
        to_output(side, result.at[:, span], (images_out.at[:, span], texts_out.at[:, span]), sems.at[i])
    for i, start in enumerate(range(0, width, COLUMNS)):
        span = pl.ds(start, COLUMNS)
        pltpu.make_async_copy(result.at[:, span], images_out.at[:, span], sems.at[i]).wait()


def last(params, y, high, low, grads, outs):
    _, rows, width = grads.shape
    return call(
        last_kernel,
        "last_pair",
        (params, y, high, low, grads, *outs),
        [VMEM] * 5 + [ANY] * 2,
        [wide(rows, width)] * 2,
        [ANY] * 2,
        12 * rows * y.shape[0] * width,
        [pltpu.VMEM((rows, width), F32), pltpu.SemaphoreType.DMA((width // COLUMNS,))],
        {5: 0, 6: 1},
    )


def after(value, *earlier):
    return lax.optimization_barrier((value, earlier))[0]


def body(images, texts, scale, bias):
    peers = lax.axis_size("dp")

    def over_link(x):
        return lax.ppermute(
            x, "dp", [(i, (i + 1) % peers if i % 2 else (i - 1) % peers) for i in range(peers)]
        )

    def on_chip(x):
        return lax.ppermute(x, "dp", [(i, i ^ 1) for i in range(peers)])

    even = is_even()
    a = jnp.where(even, images, texts)
    b = jnp.where(even, *after((texts, images), a))
    a1 = over_link(a)
    b1 = on_chip(b)
    grads, high, low, params = own(*after((images, texts), b), scale, bias)
    b1 = after(b1, grads)
    a2 = [over_link(b1[s : s + r]) for s, r in zip(offsets(SECOND), SECOND)]
    grads, bh, bl = near(params, b1, high, low, grads)
    *terms, ah, al = mate(params, bh, bl, after(a1, grads))
    terms = [on_chip(x) for x in terms]
    grads = link(params, (ah, al), high, low, grads)
    grads, *outs = far(params, after(a2[0], grads), terms, high, low, grads)
    return tuple(last(params, after(a2[1], grads), high, low, grads, outs))


def solution(mesh):
    in_specs = (P("dp", None), P("dp", None), P(), P())
    out_specs = (P("dp", None), P("dp", None))
    return jax.shard_map(body, mesh=mesh, in_specs=in_specs, out_specs=out_specs, check_vma=False)
```

```python
import functools

import jax
import jax.numpy as jnp
from jax import lax
from jax.experimental import pallas as pl
from jax.experimental.pallas import tpu as pltpu
from jax.sharding import PartitionSpec as P

F32 = jnp.float32
BF16 = jnp.bfloat16
ANY = pl.BlockSpec(memory_space=pl.ANY)
HBM = pl.BlockSpec(memory_space=pltpu.HBM)
VMEM = pl.BlockSpec(memory_space=pltpu.VMEM)
VMEM_LIMIT = 20 * 1024 * 1024

HINT = 10

FIRST = (512,)
SECOND = (384, 128)
RETURN = (256, 256)
TILE = 256
COLUMNS = 384


def halves(x):
    high = x.astype(BF16)
    return high, (x - high.astype(F32)).astype(BF16)


def dot3(xs, ys, dims):
    def one(x, y):
        return lax.dot_general(x, y, (dims, ((), ())), preferred_element_type=F32)

    return one(xs[0], ys[0]) + (one(xs[0], ys[1]) + one(xs[1], ys[0]))


def sigmoid(x):
    return 1.0 / (1.0 + jnp.exp(-x))


def offsets(rows):
    starts, at = [], 0
    for r in rows:
        starts.append(at)
        at += r
    return starts


def spans(total, tile):
    return [pl.ds(start, tile) for start in range(0, total, tile)]


def wide(*shape):
    return jax.ShapeDtypeStruct(shape, F32)


def thin(*shape):
    return jax.ShapeDtypeStruct(shape, BF16)


def call(kernel, name, args, in_specs, out_shape, out_specs, flops, scratch=(), aliases=None):
    return pl.pallas_call(
        kernel,
        out_shape=out_shape,
        in_specs=in_specs,
        out_specs=out_specs,
        scratch_shapes=list(scratch),
        input_output_aliases=aliases or {},
        compiler_params=pltpu.CompilerParams(vmem_limit_bytes=VMEM_LIMIT),
        cost_estimate=pl.CostEstimate(flops=flops, bytes_accessed=4 * 1024 * 1024, transcendentals=512 * 512),
        name=name,
    )(*args)


def joined(parts, axis):
    return jnp.concatenate(parts, axis=axis)


def one_dot(x, y, dims):
    return lax.dot_general(x, y, (dims, ((), ())), preferred_element_type=F32)


def scores(xs, ys):
    (xh, xl), (yh, yl) = xs, ys
    return one_dot(joined([xh, xh, xl], 1), joined([yh, yl, yh], 1), ((1,), (1,)))


def weighted(cs, ys):
    (ch, cl), (yh, yl) = cs, ys
    return one_dot(joined([ch, ch, cl], 1), joined([yh, yl, yh], 0), ((1,), (0,)))


def coefs(xs, ys, params):
    scale, bias = params[0:1, 0:1], params[8:9, 0:1]
    return halves(scale * sigmoid(scale * scores(xs, ys) + bias))


def term(xs, ys, params):
    return weighted(coefs(xs, ys, params), ys)


LINK, CHIP = 0, 1


def by_parity(link_is_images, link_is_texts):
    even = lax.rem(lax.axis_index("dp"), 2) == 0
    pl.when(even)(link_is_images)
    pl.when(jnp.logical_not(even))(link_is_texts)


def to_output(side, source, images, texts, sem):
    first, second = (images, texts) if side == LINK else (texts, images)
    by_parity(
        pltpu.make_async_copy(source, first, sem).start,
        pltpu.make_async_copy(source, second, sem).start,
    )


def pick_kernel(side, start, images, texts, *refs):
    out, sem = refs[-2:]
    span = pl.ds(start, out.shape[0])
    first, second = (images, texts) if side == LINK else (texts, images)
    by_parity(
        pltpu.make_async_copy(first.at[span], out, sem).start,
        pltpu.make_async_copy(second.at[span], out, sem).start,
    )
    pltpu.make_async_copy(images.at[span], out, sem).wait()


def in_hbm(x):
    return pltpu.with_memory_space_constraint(x, pltpu.HBM)


def pick(side, start, rows, images, texts, *earlier):
    width = images.shape[1]
    return call(
        functools.partial(pick_kernel, side, start),
        "pick",
        (in_hbm(images), in_hbm(texts), *earlier),
        [HBM] * 2 + [ANY] * len(earlier),
        wide(rows, width),
        VMEM,
        0,
        [pltpu.SemaphoreType.DMA(())],
    )


def own_kernel(scale_ref, bias_ref, chip_block, *refs):
    link_rows, (grads, high, low, params) = refs[:-4], refs[-4:]
    high[CHIP], low[CHIP] = halves(chip_block[...])
    high[LINK], low[LINK] = halves(joined([x[...] for x in link_rows], 0))
    scale, bias = scale_ref[...], bias_ref[...]
    params[0:8, :] = jnp.broadcast_to(scale, (8, 128))
    params[8:16, :] = jnp.broadcast_to(bias, (8, 128))
    ys = (high[CHIP], low[CHIP])
    for t, span in enumerate(spans(chip_block.shape[0], TILE)):
        xs = (high[LINK, span, :], low[LINK, span, :])
        logits = scale * scores(xs, ys) + bias
        shape = logits.shape
        diagonal = lax.broadcasted_iota(jnp.int32, shape, 0) + t * TILE == (
            lax.broadcasted_iota(jnp.int32, shape, 1)
        )
        sign = jnp.where(diagonal, -1.0, 1.0).astype(F32)
        coef = halves(sign * scale * sigmoid(sign * logits))
        grads[LINK, span, :] = weighted(coef, ys)
        part = dot3(coef, xs, ((0,), (0,)))
        grads[CHIP] = part if t == 0 else grads[CHIP] + part


def own(link_rows, chip_block, scale, bias):
    rows, width = chip_block.shape
    return call(
        own_kernel,
        "own_pair",
        (scale.reshape(1, 1), bias.reshape(1, 1), chip_block, *link_rows),
        [VMEM] * (3 + len(link_rows)),
        [wide(2, rows, width), thin(2, rows, width), thin(2, rows, width), wide(16, 128)],
        [VMEM] * 4,
        HINT * 18 * rows * rows * width,
    )


def near_kernel(params, y, high, low, grads, grads_out, yh, yl):
    ys = halves(y[...])
    yh[...], yl[...] = ys
    for span in spans(y.shape[0], TILE):
        xs = (high[CHIP, span, :], low[CHIP, span, :])
        grads_out[CHIP, span, :] = grads[CHIP, span, :] + term(xs, ys, params)


def near(params, y, high, low, grads):
    rows, width = y.shape
    return call(
        near_kernel,
        "near_pair",
        (params, y, high, low, grads),
        [VMEM] * 5,
        [wide(2, rows, width)] + [thin(rows, width)] * 2,
        [VMEM] * 3,
        12 * rows * rows * width,
        aliases={4: 0},
    )


def mate_kernel(ny, params, xh, xl, *refs):
    received, outs, (yh, yl) = refs[:ny], refs[ny:-2], refs[-2:]
    ys = halves(joined([y[...] for y in received], 0))
    yh[...], yl[...] = ys
    for start, out in zip(offsets([out.shape[0] for out in outs]), outs):
        span = pl.ds(start, out.shape[0])
        out[...] = term((xh[span, :], xl[span, :]), ys, params)


def mate(params, xh, xl, ys):
    rows, width = xh.shape
    return call(
        functools.partial(mate_kernel, len(ys)),
        "mate_pair",
        (params, xh, xl, *ys),
        [VMEM] * (3 + len(ys)),
        [wide(r, width) for r in RETURN] + [thin(rows, width)] * 2,
        [VMEM] * (len(RETURN) + 2),
        12 * rows * rows * width,
    )


def link_kernel(params, yh, yl, high, low, grads, grads_out):
    ys = (yh[...], yl[...])
    for span in spans(yh.shape[0], TILE):
        xs = (high[LINK, span, :], low[LINK, span, :])
        grads_out[LINK, span, :] = grads[LINK, span, :] + term(xs, ys, params)


def link(params, ys, high, low, grads):
    _, rows, width = grads.shape
    return call(
        link_kernel,
        "link_pair",
        (params, *ys, high, low, grads),
        [VMEM] * 6,
        wide(2, rows, width),
        VMEM,
        12 * rows * rows * width,
        aliases={5: 0},
    )


def far_kernel(nr, params, y, *refs):
    terms, (high, low, grads, grads_out, images_out, texts_out, result, sems) = refs[:nr], refs[nr:]
    starts = offsets([piece.shape[0] for piece in terms])
    for i, (start, piece) in enumerate(zip(starts, terms)):
        span = pl.ds(start, piece.shape[0])
        result[span, :] = grads[CHIP, span, :] + piece[...]
        to_output(CHIP, result.at[span], images_out.at[span], texts_out.at[span], sems.at[i])
    ys = halves(y[...])
    for span in spans(grads.shape[1], TILE):
        xs = (high[LINK, span, :], low[LINK, span, :])
        grads_out[LINK, span, :] = grads[LINK, span, :] + term(xs, ys, params)
    for i, (start, piece) in enumerate(zip(starts, terms)):
        span = pl.ds(start, piece.shape[0])
        pltpu.make_async_copy(result.at[span], images_out.at[span], sems.at[i]).wait()


def far(params, y, terms, high, low, grads):
    _, rows, width = grads.shape
    first = 2 + len(terms) + 2
    return call(
        functools.partial(far_kernel, len(terms)),
        "far_pair",
        (params, y, *terms, high, low, grads),
        [VMEM] * (first + 1),
        [wide(2, rows, width)] + [wide(rows, width)] * 2,
        [VMEM, ANY, ANY],
        12 * rows * y.shape[0] * width,
        [pltpu.VMEM((rows, width), F32), pltpu.SemaphoreType.DMA((len(terms),))],
        {first: 0},
    )


def last_kernel(params, y, high, low, grads, images_in, texts_in, images_out, texts_out, result, sems):
    yh, yl = halves(y[...])
    depth, width = y.shape
    xh, xl = high[LINK], low[LINK]
    both = one_dot(xh, joined([yh, yl], 0), ((1,), (1,)))
    total = both[:, :depth] + both[:, depth:] + one_dot(xl, yh, ((1,), (1,)))
    scale, bias = params[0:1, 0:1], params[8:9, 0:1]
    ch, cl = halves(scale * sigmoid(scale * total + bias))
    cs = joined([ch, cl, ch], 1)
    for i, start in enumerate(range(0, width, COLUMNS)):
        span = pl.ds(start, COLUMNS)
        yc = joined([yh[:, start : start + COLUMNS]] * 2 + [yl[:, start : start + COLUMNS]], 0)
        result[:, span] = grads[LINK, :, span] + one_dot(cs, yc, ((1,), (0,)))
        to_output(LINK, result.at[:, span], images_out.at[:, span], texts_out.at[:, span], sems.at[i])
    for i, start in enumerate(range(0, width, COLUMNS)):
        span = pl.ds(start, COLUMNS)
        pltpu.make_async_copy(result.at[:, span], images_out.at[:, span], sems.at[i]).wait()


def last(params, y, high, low, grads, outs):
    _, rows, width = grads.shape
    return call(
        last_kernel,
        "last_pair",
        (params, y, high, low, grads, *outs),
        [VMEM] * 5 + [ANY] * 2,
        [wide(rows, width)] * 2,
        [ANY] * 2,
        12 * rows * y.shape[0] * width,
        [pltpu.VMEM((rows, width), F32), pltpu.SemaphoreType.DMA((width // COLUMNS,))],
        {5: 0, 6: 1},
    )


def after(value, *earlier):
    return lax.optimization_barrier((value, earlier))[0]


def body(images, texts, scale, bias):
    peers = lax.axis_size("dp")

    def over_link(x):
        return lax.ppermute(
            x, "dp", [(i, (i + 1) % peers if i % 2 else (i - 1) % peers) for i in range(peers)]
        )

    def on_chip(x):
        return lax.ppermute(x, "dp", [(i, i ^ 1) for i in range(peers)])

    a = []
    for s, r in zip(offsets(FIRST), FIRST):
        a.append(pick(LINK, s, r, images, texts, *a))
    b = pick(CHIP, 0, images.shape[0], images, texts, *a)
    a1 = [over_link(x) for x in a]
    b1 = on_chip(b)
    grads, high, low, params = own(a, b, scale, bias)
    b1 = after(b1, grads)
    a2 = [over_link(b1[s : s + r]) for s, r in zip(offsets(SECOND), SECOND)]
    grads, bh, bl = near(params, b1, high, low, grads)
    *terms, ah, al = mate(params, bh, bl, after(a1, grads))
    terms = [on_chip(x) for x in terms]
    grads = link(params, (ah, al), high, low, grads)
    grads, *outs = far(params, after(a2[0], grads), terms, high, low, grads)
    return tuple(last(params, after(a2[1], grads), high, low, grads, outs))


def solution(mesh):
    in_specs = (P("dp", None), P("dp", None), P(), P())
    out_specs = (P("dp", None), P("dp", None))
    return jax.shard_map(body, mesh=mesh, in_specs=in_specs, out_specs=out_specs, check_vma=False)
```

```python
import functools

import jax
import jax.numpy as jnp
from jax import lax
from jax.experimental import pallas as pl
from jax.experimental.pallas import tpu as pltpu
from jax.sharding import PartitionSpec as P

F32 = jnp.float32
BF16 = jnp.bfloat16
ANY = pl.BlockSpec(memory_space=pl.ANY)
HBM = pl.BlockSpec(memory_space=pltpu.HBM)
VMEM = pl.BlockSpec(memory_space=pltpu.VMEM)
VMEM_LIMIT = 20 * 1024 * 1024

HINT = 10

HEAD = 256
SECOND = (384, 128)
RETURN = (256, 256)
TILE = 256
COLUMNS = 384


def halves(x):
    high = x.astype(BF16)
    return high, (x - high.astype(F32)).astype(BF16)


def dot3(xs, ys, dims):
    def one(x, y):
        return lax.dot_general(x, y, (dims, ((), ())), preferred_element_type=F32)

    return one(xs[0], ys[0]) + (one(xs[0], ys[1]) + one(xs[1], ys[0]))


def sigmoid(x):
    return 1.0 / (1.0 + jnp.exp(-x))


def offsets(rows):
    starts, at = [], 0
    for r in rows:
        starts.append(at)
        at += r
    return starts


def spans(total, tile):
    return [pl.ds(start, tile) for start in range(0, total, tile)]


def wide(*shape):
    return jax.ShapeDtypeStruct(shape, F32)


def thin(*shape):
    return jax.ShapeDtypeStruct(shape, BF16)


def call(kernel, name, args, in_specs, out_shape, out_specs, flops, scratch=(), aliases=None):
    return pl.pallas_call(
        kernel,
        out_shape=out_shape,
        in_specs=in_specs,
        out_specs=out_specs,
        scratch_shapes=list(scratch),
        input_output_aliases=aliases or {},
        compiler_params=pltpu.CompilerParams(vmem_limit_bytes=VMEM_LIMIT),
        cost_estimate=pl.CostEstimate(flops=flops, bytes_accessed=4 * 1024 * 1024, transcendentals=512 * 512),
        name=name,
    )(*args)


def joined(parts, axis):
    return jnp.concatenate(parts, axis=axis)


def one_dot(x, y, dims):
    return lax.dot_general(x, y, (dims, ((), ())), preferred_element_type=F32)


def scores(xs, ys):
    (xh, xl), (yh, yl) = xs, ys
    return one_dot(joined([xh, xh, xl], 1), joined([yh, yl, yh], 1), ((1,), (1,)))


def weighted(cs, ys):
    (ch, cl), (yh, yl) = cs, ys
    return one_dot(joined([ch, ch, cl], 1), joined([yh, yl, yh], 0), ((1,), (0,)))


def coefs(xs, ys, params):
    scale, bias = params[0:1, 0:1], params[8:9, 0:1]
    return halves(scale * sigmoid(scale * scores(xs, ys) + bias))


def term(xs, ys, params):
    return weighted(coefs(xs, ys, params), ys)


LINK, CHIP = 0, 1


def by_parity(link_is_images, link_is_texts):
    even = lax.rem(lax.axis_index("dp"), 2) == 0
    pl.when(even)(link_is_images)
    pl.when(jnp.logical_not(even))(link_is_texts)


def to_output(side, source, images, texts, sem):
    first, second = (images, texts) if side == LINK else (texts, images)
    by_parity(
        pltpu.make_async_copy(source, first, sem).start,
        pltpu.make_async_copy(source, second, sem).start,
    )


def pick_kernel(parts, images, texts, *refs):
    outs, sems = refs[-1 - len(parts) : -1], refs[-1]
    for k, ((side, start, rows), out) in enumerate(zip(parts, outs)):
        span = pl.ds(start, rows)
        first, second = (images, texts) if side == LINK else (texts, images)
        by_parity(
            pltpu.make_async_copy(first.at[span], out, sems.at[k]).start,
            pltpu.make_async_copy(second.at[span], out, sems.at[k]).start,
        )
    for k, ((_, start, rows), out) in enumerate(zip(parts, outs)):
        pltpu.make_async_copy(images.at[pl.ds(start, rows)], out, sems.at[k]).wait()


def in_hbm(x):
    return pltpu.with_memory_space_constraint(x, pltpu.HBM)


def pick(images, texts, parts, *earlier):
    width = images.shape[1]
    return call(
        functools.partial(pick_kernel, parts),
        "pick",
        (in_hbm(images), in_hbm(texts), *earlier),
        [HBM] * 2 + [ANY] * len(earlier),
        [wide(rows, width) for _, _, rows in parts],
        [VMEM] * len(parts),
        0,
        [pltpu.SemaphoreType.DMA((len(parts),))],
    )


def own_kernel(scale_ref, bias_ref, chip_block, *refs):
    link_rows, (grads, high, low, params) = refs[:-4], refs[-4:]
    high[CHIP], low[CHIP] = halves(chip_block[...])
    high[LINK], low[LINK] = halves(joined([x[...] for x in link_rows], 0))
    scale, bias = scale_ref[...], bias_ref[...]
    params[0:8, :] = jnp.broadcast_to(scale, (8, 128))
    params[8:16, :] = jnp.broadcast_to(bias, (8, 128))
    ys = (high[CHIP], low[CHIP])
    for t, span in enumerate(spans(chip_block.shape[0], TILE)):
        xs = (high[LINK, span, :], low[LINK, span, :])
        logits = scale * scores(xs, ys) + bias
        shape = logits.shape
        diagonal = lax.broadcasted_iota(jnp.int32, shape, 0) + t * TILE == (
            lax.broadcasted_iota(jnp.int32, shape, 1)
        )
        sign = jnp.where(diagonal, -1.0, 1.0).astype(F32)
        coef = halves(sign * scale * sigmoid(sign * logits))
        grads[LINK, span, :] = weighted(coef, ys)
        part = dot3(coef, xs, ((0,), (0,)))
        grads[CHIP] = part if t == 0 else grads[CHIP] + part


def own(link_rows, chip_block, scale, bias):
    rows, width = chip_block.shape
    return call(
        own_kernel,
        "own_pair",
        (scale.reshape(1, 1), bias.reshape(1, 1), chip_block, *link_rows),
        [VMEM] * (3 + len(link_rows)),
        [wide(2, rows, width), thin(2, rows, width), thin(2, rows, width), wide(16, 128)],
        [VMEM] * 4,
        HINT * 18 * rows * rows * width,
    )


def near_kernel(params, y, high, low, grads, grads_out, yh, yl):
    ys = halves(y[...])
    yh[...], yl[...] = ys
    for span in spans(y.shape[0], TILE):
        xs = (high[CHIP, span, :], low[CHIP, span, :])
        grads_out[CHIP, span, :] = grads[CHIP, span, :] + term(xs, ys, params)


def near(params, y, high, low, grads):
    rows, width = y.shape
    return call(
        near_kernel,
        "near_pair",
        (params, y, high, low, grads),
        [VMEM] * 5,
        [wide(2, rows, width)] + [thin(rows, width)] * 2,
        [VMEM] * 3,
        12 * rows * rows * width,
        aliases={4: 0},
    )


def mate_kernel(ny, params, xh, xl, *refs):
    received, outs, (yh, yl) = refs[:ny], refs[ny:-2], refs[-2:]
    ys = halves(joined([y[...] for y in received], 0))
    yh[...], yl[...] = ys
    for start, out in zip(offsets([out.shape[0] for out in outs]), outs):
        span = pl.ds(start, out.shape[0])
        out[...] = term((xh[span, :], xl[span, :]), ys, params)


def mate(params, xh, xl, ys):
    rows, width = xh.shape
    return call(
        functools.partial(mate_kernel, len(ys)),
        "mate_pair",
        (params, xh, xl, *ys),
        [VMEM] * (3 + len(ys)),
        [wide(r, width) for r in RETURN] + [thin(rows, width)] * 2,
        [VMEM] * (len(RETURN) + 2),
        12 * rows * rows * width,
    )


def link_kernel(params, yh, yl, high, low, grads, grads_out):
    ys = (yh[...], yl[...])
    for span in spans(yh.shape[0], TILE):
        xs = (high[LINK, span, :], low[LINK, span, :])
        grads_out[LINK, span, :] = grads[LINK, span, :] + term(xs, ys, params)


def link(params, ys, high, low, grads):
    _, rows, width = grads.shape
    return call(
        link_kernel,
        "link_pair",
        (params, *ys, high, low, grads),
        [VMEM] * 6,
        wide(2, rows, width),
        VMEM,
        12 * rows * rows * width,
        aliases={5: 0},
    )


def far_kernel(nr, params, y, *refs):
    terms, (high, low, grads, grads_out, images_out, texts_out, result, sems) = refs[:nr], refs[nr:]
    starts = offsets([piece.shape[0] for piece in terms])
    for i, (start, piece) in enumerate(zip(starts, terms)):
        span = pl.ds(start, piece.shape[0])
        result[span, :] = grads[CHIP, span, :] + piece[...]
        to_output(CHIP, result.at[span], images_out.at[span], texts_out.at[span], sems.at[i])
    ys = halves(y[...])
    for span in spans(grads.shape[1], TILE):
        xs = (high[LINK, span, :], low[LINK, span, :])
        grads_out[LINK, span, :] = grads[LINK, span, :] + term(xs, ys, params)
    for i, (start, piece) in enumerate(zip(starts, terms)):
        span = pl.ds(start, piece.shape[0])
        pltpu.make_async_copy(result.at[span], images_out.at[span], sems.at[i]).wait()


def far(params, y, terms, high, low, grads):
    _, rows, width = grads.shape
    first = 2 + len(terms) + 2
    return call(
        functools.partial(far_kernel, len(terms)),
        "far_pair",
        (params, y, *terms, high, low, grads),
        [VMEM] * (first + 1),
        [wide(2, rows, width)] + [wide(rows, width)] * 2,
        [VMEM, ANY, ANY],
        12 * rows * y.shape[0] * width,
        [pltpu.VMEM((rows, width), F32), pltpu.SemaphoreType.DMA((len(terms),))],
        {first: 0},
    )


def last_kernel(params, y, high, low, grads, images_in, texts_in, images_out, texts_out, result, sems):
    yh, yl = halves(y[...])
    depth, width = y.shape
    xh, xl = high[LINK], low[LINK]
    both = one_dot(xh, joined([yh, yl], 0), ((1,), (1,)))
    total = both[:, :depth] + both[:, depth:] + one_dot(xl, yh, ((1,), (1,)))
    scale, bias = params[0:1, 0:1], params[8:9, 0:1]
    ch, cl = halves(scale * sigmoid(scale * total + bias))
    cs = joined([ch, cl, ch], 1)
    for i, start in enumerate(range(0, width, COLUMNS)):
        span = pl.ds(start, COLUMNS)
        yc = joined([yh[:, start : start + COLUMNS]] * 2 + [yl[:, start : start + COLUMNS]], 0)
        result[:, span] = grads[LINK, :, span] + one_dot(cs, yc, ((1,), (0,)))
        to_output(LINK, result.at[:, span], images_out.at[:, span], texts_out.at[:, span], sems.at[i])
    for i, start in enumerate(range(0, width, COLUMNS)):
        span = pl.ds(start, COLUMNS)
        pltpu.make_async_copy(result.at[:, span], images_out.at[:, span], sems.at[i]).wait()


def last(params, y, high, low, grads, outs):
    _, rows, width = grads.shape
    return call(
        last_kernel,
        "last_pair",
        (params, y, high, low, grads, *outs),
        [VMEM] * 5 + [ANY] * 2,
        [wide(rows, width)] * 2,
        [ANY] * 2,
        12 * rows * y.shape[0] * width,
        [pltpu.VMEM((rows, width), F32), pltpu.SemaphoreType.DMA((width // COLUMNS,))],
        {5: 0, 6: 1},
    )


def after(value, *earlier):
    return lax.optimization_barrier((value, earlier))[0]


def body(images, texts, scale, bias):
    peers = lax.axis_size("dp")

    def over_link(x):
        return lax.ppermute(
            x, "dp", [(i, (i + 1) % peers if i % 2 else (i - 1) % peers) for i in range(peers)]
        )

    def on_chip(x):
        return lax.ppermute(x, "dp", [(i, i ^ 1) for i in range(peers)])

    rows = images.shape[0]
    head = pick(images, texts, [(LINK, 0, HEAD)])
    tail, b = pick(images, texts, [(LINK, HEAD, rows - HEAD), (CHIP, 0, rows)], *head)
    a = [*head, tail]
    a1 = [over_link(x) for x in a]
    b1 = on_chip(b)
    grads, high, low, params = own(a, b, scale, bias)
    b1 = after(b1, grads)
    a2 = [over_link(b1[s : s + r]) for s, r in zip(offsets(SECOND), SECOND)]
    grads, bh, bl = near(params, b1, high, low, grads)
    *terms, ah, al = mate(params, bh, bl, after(a1, grads))
    terms = [on_chip(x) for x in terms]
    grads = link(params, (ah, al), high, low, grads)
    grads, *outs = far(params, after(a2[0], grads), terms, high, low, grads)
    return tuple(last(params, after(a2[1], grads), high, low, grads, outs))


def solution(mesh):
    in_specs = (P("dp", None), P("dp", None), P(), P())
    out_specs = (P("dp", None), P("dp", None))
    return jax.shard_map(body, mesh=mesh, in_specs=in_specs, out_specs=out_specs, check_vma=False)
```

```python
import functools

import jax
import jax.numpy as jnp
from jax import lax
from jax.experimental import pallas as pl
from jax.experimental.pallas import tpu as pltpu
from jax.sharding import PartitionSpec as P

F32 = jnp.float32
BF16 = jnp.bfloat16
ANY = pl.BlockSpec(memory_space=pl.ANY)
HBM = pl.BlockSpec(memory_space=pltpu.HBM)
VMEM = pl.BlockSpec(memory_space=pltpu.VMEM)
VMEM_LIMIT = 20 * 1024 * 1024

HINT = 10

HEAD = 256
HEAD_TERMS = (256,)
TAIL_TERMS = (112, 144)
TILE = 256


def halves(x):
    high = x.astype(BF16)
    return high, (x - high.astype(F32)).astype(BF16)


def dot3(xs, ys, dims):
    def one(x, y):
        return lax.dot_general(x, y, (dims, ((), ())), preferred_element_type=F32)

    return one(xs[0], ys[0]) + (one(xs[0], ys[1]) + one(xs[1], ys[0]))


def sigmoid(x):
    return 1.0 / (1.0 + jnp.exp(-x))


def offsets(rows):
    starts, at = [], 0
    for r in rows:
        starts.append(at)
        at += r
    return starts


def spans(total, tile):
    return [pl.ds(start, tile) for start in range(0, total, tile)]


def wide(*shape):
    return jax.ShapeDtypeStruct(shape, F32)


def thin(*shape):
    return jax.ShapeDtypeStruct(shape, BF16)


def call(kernel, name, args, in_specs, out_shape, out_specs, flops, scratch=(), aliases=None):
    return pl.pallas_call(
        kernel,
        out_shape=out_shape,
        in_specs=in_specs,
        out_specs=out_specs,
        scratch_shapes=list(scratch),
        input_output_aliases=aliases or {},
        compiler_params=pltpu.CompilerParams(vmem_limit_bytes=VMEM_LIMIT),
        cost_estimate=pl.CostEstimate(flops=flops, bytes_accessed=4 * 1024 * 1024, transcendentals=512 * 512),
        name=name,
    )(*args)


def joined(parts, axis):
    return jnp.concatenate(parts, axis=axis)


def one_dot(x, y, dims):
    return lax.dot_general(x, y, (dims, ((), ())), preferred_element_type=F32)


def scores(xs, ys):
    (xh, xl), (yh, yl) = xs, ys
    return one_dot(joined([xh, xh, xl], 1), joined([yh, yl, yh], 1), ((1,), (1,)))


def weighted(cs, ys):
    (ch, cl), (yh, yl) = cs, ys
    return one_dot(joined([ch, ch, cl], 1), joined([yh, yl, yh], 0), ((1,), (0,)))


def coefs(xs, ys, params):
    scale, bias = params[0:1, 0:1], params[8:9, 0:1]
    return halves(scale * sigmoid(scale * scores(xs, ys) + bias))


def term(xs, ys, params):
    return weighted(coefs(xs, ys, params), ys)


LINK, CHIP = 0, 1


def by_parity(link_is_images, link_is_texts):
    even = lax.rem(lax.axis_index("dp"), 2) == 0
    pl.when(even)(link_is_images)
    pl.when(jnp.logical_not(even))(link_is_texts)


def to_output(side, source, images, texts, sem):
    first, second = (images, texts) if side == LINK else (texts, images)
    by_parity(
        pltpu.make_async_copy(source, first, sem).start,
        pltpu.make_async_copy(source, second, sem).start,
    )


def pick_kernel(parts, images, texts, *refs):
    outs, sems = refs[-1 - len(parts) : -1], refs[-1]
    for k, ((side, start, rows), out) in enumerate(zip(parts, outs)):
        span = pl.ds(start, rows)
        first, second = (images, texts) if side == LINK else (texts, images)
        by_parity(
            pltpu.make_async_copy(first.at[span], out, sems.at[k]).start,
            pltpu.make_async_copy(second.at[span], out, sems.at[k]).start,
        )
    for k, ((_, start, rows), out) in enumerate(zip(parts, outs)):
        pltpu.make_async_copy(images.at[pl.ds(start, rows)], out, sems.at[k]).wait()


def in_hbm(x):
    return pltpu.with_memory_space_constraint(x, pltpu.HBM)


def pick(images, texts, parts, *earlier):
    width = images.shape[1]
    return call(
        functools.partial(pick_kernel, parts),
        "pick",
        (in_hbm(images), in_hbm(texts), *earlier),
        [HBM] * 2 + [ANY] * len(earlier),
        [wide(rows, width) for _, _, rows in parts],
        [VMEM] * len(parts),
        0,
        [pltpu.SemaphoreType.DMA((len(parts),))],
    )


def own_kernel(scale_ref, bias_ref, chip_block, *refs):
    link_rows, (grads, high, low, params) = refs[:-4], refs[-4:]
    high[CHIP], low[CHIP] = halves(chip_block[...])
    high[LINK], low[LINK] = halves(joined([x[...] for x in link_rows], 0))
    scale, bias = scale_ref[...], bias_ref[...]
    params[0:8, :] = jnp.broadcast_to(scale, (8, 128))
    params[8:16, :] = jnp.broadcast_to(bias, (8, 128))
    ys = (high[CHIP], low[CHIP])
    for t, span in enumerate(spans(chip_block.shape[0], TILE)):
        xs = (high[LINK, span, :], low[LINK, span, :])
        logits = scale * scores(xs, ys) + bias
        shape = logits.shape
        diagonal = lax.broadcasted_iota(jnp.int32, shape, 0) + t * TILE == (
            lax.broadcasted_iota(jnp.int32, shape, 1)
        )
        sign = jnp.where(diagonal, -1.0, 1.0).astype(F32)
        coef = halves(sign * scale * sigmoid(sign * logits))
        grads[LINK, span, :] = weighted(coef, ys)
        part = dot3(coef, xs, ((0,), (0,)))
        grads[CHIP] = part if t == 0 else grads[CHIP] + part


def own(link_rows, chip_block, scale, bias):
    rows, width = chip_block.shape
    return call(
        own_kernel,
        "own_pair",
        (scale.reshape(1, 1), bias.reshape(1, 1), chip_block, *link_rows),
        [VMEM] * (3 + len(link_rows)),
        [wide(2, rows, width), thin(2, rows, width), thin(2, rows, width), wide(16, 128)],
        [VMEM] * 4,
        HINT * 18 * rows * rows * width,
    )


def both_kernel(first, params, x, *refs):
    if first:
        y, mate, high, low, yh, yl, *terms = refs
        yh[...], yl[...] = halves(y[...])
    else:
        yh, yl, before, mate, high, low, *terms = refs
    ys = (yh[...], yl[...])
    xs = halves(x[...])
    high[...], low[...] = xs
    coef = coefs(xs, ys, params)
    start = 0
    for term_out in terms:
        rows = term_out.shape[0]
        term_out[...] = weighted([c[start : start + rows] for c in coef], ys)
        start += rows
    part = dot3(coef, xs, ((0,), (0,)))
    mate[...] = part if first else before[...] + part


def both_terms(params, x, pieces, y=None, ys=(), before=None):
    depth, width = x.shape
    first = y is not None
    inputs = (params, x, y) if first else (params, x, *ys, before)
    rows = inputs[-1].shape[0]
    outs = [wide(rows, width), thin(depth, width), thin(depth, width)]
    outs += [thin(rows, width)] * 2 if first else []
    outs += [wide(r, width) for r in pieces]
    return call(
        functools.partial(both_kernel, first),
        "both_terms",
        inputs,
        [VMEM] * len(inputs),
        outs,
        [VMEM] * len(outs),
        18 * rows * depth * width,
        aliases={} if first else {4: 0},
    )


def add_kernel(side, pieces, params, *refs):
    highs, lows, (high, low, grads, grads_out) = refs[:pieces], refs[pieces : 2 * pieces], refs[2 * pieces :]
    ys = tuple(joined([y[...] for y in part], 0) if pieces > 1 else part[0][...] for part in (highs, lows))
    for span in spans(grads.shape[1], TILE):
        xs = (high[side, span, :], low[side, span, :])
        grads_out[side, span, :] = grads[side, span, :] + term(xs, ys, params)


def add_term(side, params, highs, lows, high, low, grads, hint=1):
    _, rows, width = grads.shape
    pieces = len(highs)
    last = 3 + 2 * pieces
    return call(
        functools.partial(add_kernel, side, pieces),
        "add_term",
        (params, *highs, *lows, high, low, grads),
        [VMEM] * (last + 1),
        wide(2, rows, width),
        VMEM,
        hint * 12 * rows * rows * width,
        aliases={last: 0},
    )


def finish_kernel(side, start, term_in, grads, *refs):
    images_out, texts_out, result, sem = refs[-4:]
    span = pl.ds(start, term_in.shape[0])
    result[...] = grads[side, span, :] + term_in[...]
    to_output(side, result, images_out.at[span], texts_out.at[span], sem)
    pltpu.make_async_copy(result, images_out.at[span], sem).wait()


def finish(side, start, term_in, grads, outs=()):
    _, rows, width = grads.shape
    return call(
        functools.partial(finish_kernel, side, start),
        "finish",
        (term_in, grads, *outs),
        [VMEM] * 2 + [ANY] * len(outs),
        [wide(rows, width)] * 2,
        [ANY] * 2,
        0,
        [pltpu.VMEM(term_in.shape, F32), pltpu.SemaphoreType.DMA(())],
        {2 + i: i for i in range(len(outs))},
    )


def after(value, *earlier):
    return lax.optimization_barrier((value, earlier))[0]


def body(images, texts, scale, bias):
    peers = lax.axis_size("dp")

    def over_link(x):
        return lax.ppermute(
            x, "dp", [(i, (i + 1) % peers if i % 2 else (i - 1) % peers) for i in range(peers)]
        )

    def on_chip(x):
        return lax.ppermute(x, "dp", [(i, i ^ 1) for i in range(peers)])

    rows = images.shape[0]
    head = pick(images, texts, [(LINK, 0, HEAD)])
    tail, b = pick(images, texts, [(LINK, HEAD, rows - HEAD), (CHIP, 0, rows)], *head)
    a = [*head, tail]
    a1 = [over_link(x) for x in a]
    b1 = on_chip(b)
    grads, high, low, params = own(a, b, scale, bias)
    b1, head1 = after((b1, a1[0]), grads)
    mate, ah, al, bh, bl, *terms = both_terms(params, head1, HEAD_TERMS, y=b1)
    returned = [over_link(x) for x in terms]
    grads = add_term(CHIP, params, [bh], [bl], high, low, grads)
    mate, th, tl, *terms = both_terms(params, after(a1[1], grads), TAIL_TERMS, ys=(bh, bl), before=mate)
    returned += [over_link(x) for x in terms]
    mate = on_chip(mate)
    grads = add_term(LINK, params, [after(ah, returned[0]), th], [al, tl], high, low, grads, HINT)
    outs = finish(CHIP, 0, after(mate, grads), grads)
    start = 0
    for piece in returned:
        outs = finish(LINK, start, after(piece, outs), grads, outs)
        start += piece.shape[0]
    return tuple(outs)


def solution(mesh):
    in_specs = (P("dp", None), P("dp", None), P(), P())
    out_specs = (P("dp", None), P("dp", None))
    return jax.shard_map(body, mesh=mesh, in_specs=in_specs, out_specs=out_specs, check_vma=False)
```

```python
import functools

import jax
import jax.numpy as jnp
from jax import lax
from jax.experimental import pallas as pl
from jax.experimental.pallas import tpu as pltpu
from jax.sharding import PartitionSpec as P

F32 = jnp.float32
BF16 = jnp.bfloat16
ANY = pl.BlockSpec(memory_space=pl.ANY)
HBM = pl.BlockSpec(memory_space=pltpu.HBM)
VMEM = pl.BlockSpec(memory_space=pltpu.VMEM)
VMEM_LIMIT = 20 * 1024 * 1024

HINT = 10

HEAD = 256
HEAD_TERMS = (256,)
TAIL_TERMS = (112, 144)
TILE = 256


def halves(x):
    high = x.astype(BF16)
    return high, (x - high.astype(F32)).astype(BF16)


def dot3(xs, ys, dims):
    def one(x, y):
        return lax.dot_general(x, y, (dims, ((), ())), preferred_element_type=F32)

    return one(xs[0], ys[0]) + (one(xs[0], ys[1]) + one(xs[1], ys[0]))


def sigmoid(x):
    return 1.0 / (1.0 + jnp.exp(-x))


def offsets(rows):
    starts, at = [], 0
    for r in rows:
        starts.append(at)
        at += r
    return starts


def spans(total, tile):
    return [pl.ds(start, tile) for start in range(0, total, tile)]


def wide(*shape):
    return jax.ShapeDtypeStruct(shape, F32)


def thin(*shape):
    return jax.ShapeDtypeStruct(shape, BF16)


def call(kernel, name, args, in_specs, out_shape, out_specs, flops, scratch=(), aliases=None):
    return pl.pallas_call(
        kernel,
        out_shape=out_shape,
        in_specs=in_specs,
        out_specs=out_specs,
        scratch_shapes=list(scratch),
        input_output_aliases=aliases or {},
        compiler_params=pltpu.CompilerParams(vmem_limit_bytes=VMEM_LIMIT),
        cost_estimate=pl.CostEstimate(flops=flops, bytes_accessed=4 * 1024 * 1024, transcendentals=512 * 512),
        name=name,
    )(*args)


def joined(parts, axis):
    return jnp.concatenate(parts, axis=axis)


def one_dot(x, y, dims):
    return lax.dot_general(x, y, (dims, ((), ())), preferred_element_type=F32)


def scores(xs, ys):
    (xh, xl), (yh, yl) = xs, ys
    return one_dot(joined([xh, xh, xl], 1), joined([yh, yl, yh], 1), ((1,), (1,)))


def weighted(cs, ys):
    (ch, cl), (yh, yl) = cs, ys
    return one_dot(joined([ch, ch, cl], 1), joined([yh, yl, yh], 0), ((1,), (0,)))


def coefs(xs, ys, params):
    scale, bias = params[0:1, 0:1], params[8:9, 0:1]
    return halves(scale * sigmoid(scale * scores(xs, ys) + bias))


def term(xs, ys, params):
    return weighted(coefs(xs, ys, params), ys)


LINK, CHIP = 0, 1


def by_parity(link_is_images, link_is_texts):
    even = lax.rem(lax.axis_index("dp"), 2) == 0
    pl.when(even)(link_is_images)
    pl.when(jnp.logical_not(even))(link_is_texts)


def to_output(side, source, images, texts, sem):
    first, second = (images, texts) if side == LINK else (texts, images)
    by_parity(
        pltpu.make_async_copy(source, first, sem).start,
        pltpu.make_async_copy(source, second, sem).start,
    )


def pick_kernel(parts, images, texts, *refs):
    outs, sems = refs[-1 - len(parts) : -1], refs[-1]
    for k, ((side, start, rows), out) in enumerate(zip(parts, outs)):
        span = pl.ds(start, rows)
        first, second = (images, texts) if side == LINK else (texts, images)
        by_parity(
            pltpu.make_async_copy(first.at[span], out, sems.at[k]).start,
            pltpu.make_async_copy(second.at[span], out, sems.at[k]).start,
        )
    for k, ((_, start, rows), out) in enumerate(zip(parts, outs)):
        pltpu.make_async_copy(images.at[pl.ds(start, rows)], out, sems.at[k]).wait()


def in_hbm(x):
    return pltpu.with_memory_space_constraint(x, pltpu.HBM)


def pick(images, texts, parts, *earlier):
    width = images.shape[1]
    return call(
        functools.partial(pick_kernel, parts),
        "pick",
        (in_hbm(images), in_hbm(texts), *earlier),
        [HBM] * 2 + [ANY] * len(earlier),
        [wide(rows, width) for _, _, rows in parts],
        [VMEM] * len(parts),
        0,
        [pltpu.SemaphoreType.DMA((len(parts),))],
    )


def own_kernel(scale_ref, bias_ref, chip_block, *refs):
    link_rows, (grads, high, low, params) = refs[:-4], refs[-4:]
    high[CHIP], low[CHIP] = halves(chip_block[...])
    high[LINK], low[LINK] = halves(joined([x[...] for x in link_rows], 0))
    scale, bias = scale_ref[...], bias_ref[...]
    params[0:8, :] = jnp.broadcast_to(scale, (8, 128))
    params[8:16, :] = jnp.broadcast_to(bias, (8, 128))
    ys = (high[CHIP], low[CHIP])
    for t, span in enumerate(spans(chip_block.shape[0], TILE)):
        xs = (high[LINK, span, :], low[LINK, span, :])
        logits = scale * scores(xs, ys) + bias
        shape = logits.shape
        diagonal = lax.broadcasted_iota(jnp.int32, shape, 0) + t * TILE == (
            lax.broadcasted_iota(jnp.int32, shape, 1)
        )
        sign = jnp.where(diagonal, -1.0, 1.0).astype(F32)
        coef = halves(sign * scale * sigmoid(sign * logits))
        grads[LINK, span, :] = weighted(coef, ys)
        part = dot3(coef, xs, ((0,), (0,)))
        grads[CHIP] = part if t == 0 else grads[CHIP] + part


def own(link_rows, chip_block, scale, bias):
    rows, width = chip_block.shape
    return call(
        own_kernel,
        "own_pair",
        (scale.reshape(1, 1), bias.reshape(1, 1), chip_block, *link_rows),
        [VMEM] * (3 + len(link_rows)),
        [wide(2, rows, width), thin(2, rows, width), thin(2, rows, width), wide(16, 128)],
        [VMEM] * 4,
        HINT * 18 * rows * rows * width,
    )


def both_kernel(first, params, x, yh, yl, *refs):
    before, (mate, high, low, *terms) = (None, refs) if first else (refs[0], refs[1:])
    ys = (yh[...], yl[...])
    xs = halves(x[...])
    high[...], low[...] = xs
    coef = coefs(xs, ys, params)
    start = 0
    for term_out in terms:
        rows = term_out.shape[0]
        term_out[...] = weighted([c[start : start + rows] for c in coef], ys)
        start += rows
    part = dot3(coef, xs, ((0,), (0,)))
    mate[...] = part if first else before[...] + part


def both_terms(params, x, pieces, ys, before=None):
    depth, width = x.shape
    rows = ys[0].shape[0]
    first = before is None
    inputs = (params, x, *ys) if first else (params, x, *ys, before)
    outs = [wide(rows, width), thin(depth, width), thin(depth, width)]
    outs += [wide(r, width) for r in pieces]
    return call(
        functools.partial(both_kernel, first),
        "both_terms",
        inputs,
        [VMEM] * len(inputs),
        outs,
        [VMEM] * len(outs),
        18 * rows * depth * width,
        aliases={} if first else {4: 0},
    )


def near_kernel(params, y, high, low, grads, grads_out, yh, yl):
    ys = halves(y[...])
    yh[...], yl[...] = ys
    for span in spans(y.shape[0], TILE):
        xs = (high[CHIP, span, :], low[CHIP, span, :])
        grads_out[CHIP, span, :] = grads[CHIP, span, :] + term(xs, ys, params)


def near(params, y, high, low, grads):
    rows, width = y.shape
    return call(
        near_kernel,
        "near_pair",
        (params, y, high, low, grads),
        [VMEM] * 5,
        [wide(2, rows, width)] + [thin(rows, width)] * 2,
        [VMEM] * 3,
        12 * rows * rows * width,
        aliases={4: 0},
    )


def add_kernel(side, pieces, params, *refs):
    highs, lows, (high, low, grads, grads_out) = refs[:pieces], refs[pieces : 2 * pieces], refs[2 * pieces :]
    ys = tuple(joined([y[...] for y in part], 0) if pieces > 1 else part[0][...] for part in (highs, lows))
    for span in spans(grads.shape[1], TILE):
        xs = (high[side, span, :], low[side, span, :])
        grads_out[side, span, :] = grads[side, span, :] + term(xs, ys, params)


def add_term(side, params, highs, lows, high, low, grads, hint=1):
    _, rows, width = grads.shape
    pieces = len(highs)
    last = 3 + 2 * pieces
    return call(
        functools.partial(add_kernel, side, pieces),
        "add_term",
        (params, *highs, *lows, high, low, grads),
        [VMEM] * (last + 1),
        wide(2, rows, width),
        VMEM,
        hint * 12 * rows * rows * width,
        aliases={last: 0},
    )


def finish_kernel(side, start, term_in, grads, *refs):
    images_out, texts_out, result, sem = refs[-4:]
    span = pl.ds(start, term_in.shape[0])
    result[...] = grads[side, span, :] + term_in[...]
    to_output(side, result, images_out.at[span], texts_out.at[span], sem)
    pltpu.make_async_copy(result, images_out.at[span], sem).wait()


def finish(side, start, term_in, grads, outs=()):
    _, rows, width = grads.shape
    return call(
        functools.partial(finish_kernel, side, start),
        "finish",
        (term_in, grads, *outs),
        [VMEM] * 2 + [ANY] * len(outs),
        [wide(rows, width)] * 2,
        [ANY] * 2,
        0,
        [pltpu.VMEM(term_in.shape, F32), pltpu.SemaphoreType.DMA(())],
        {2 + i: i for i in range(len(outs))},
    )


def after(value, *earlier):
    return lax.optimization_barrier((value, earlier))[0]


def body(images, texts, scale, bias):
    peers = lax.axis_size("dp")

    def over_link(x):
        return lax.ppermute(
            x, "dp", [(i, (i + 1) % peers if i % 2 else (i - 1) % peers) for i in range(peers)]
        )

    def on_chip(x):
        return lax.ppermute(x, "dp", [(i, i ^ 1) for i in range(peers)])

    rows = images.shape[0]
    head = pick(images, texts, [(LINK, 0, HEAD)])
    tail, b = pick(images, texts, [(LINK, HEAD, rows - HEAD), (CHIP, 0, rows)], *head)
    a = [*head, tail]
    a1 = [over_link(x) for x in a]
    b1 = on_chip(b)
    grads, high, low, params = own(a, b, scale, bias)
    grads, *ys = near(params, after(b1, grads), high, low, grads)
    mate, ah, al, *terms = both_terms(params, after(a1[0], grads), HEAD_TERMS, ys)
    returned = [over_link(x) for x in terms]
    mate, th, tl, *terms = both_terms(params, after(a1[1], mate), TAIL_TERMS, ys, mate)
    returned += [over_link(x) for x in terms]
    mate = on_chip(mate)
    grads = add_term(LINK, params, [after(ah, returned[0]), th], [al, tl], high, low, grads, HINT)
    outs = finish(CHIP, 0, after(mate, grads), grads)
    start = 0
    for piece in returned:
        outs = finish(LINK, start, after(piece, outs), grads, outs)
        start += piece.shape[0]
    return tuple(outs)


def solution(mesh):
    in_specs = (P("dp", None), P("dp", None), P(), P())
    out_specs = (P("dp", None), P("dp", None))
    return jax.shard_map(body, mesh=mesh, in_specs=in_specs, out_specs=out_specs, check_vma=False)
```

```python
import functools

import jax
import jax.numpy as jnp
from jax import lax
from jax.experimental import pallas as pl
from jax.experimental.pallas import tpu as pltpu
from jax.sharding import PartitionSpec as P

F32 = jnp.float32
BF16 = jnp.bfloat16
ANY = pl.BlockSpec(memory_space=pl.ANY)
HBM = pl.BlockSpec(memory_space=pltpu.HBM)
VMEM = pl.BlockSpec(memory_space=pltpu.VMEM)
VMEM_LIMIT = 20 * 1024 * 1024

HINT = 10

HEAD = 256
HEAD_TERMS = (256,)
TAIL_TERMS = (256,)
TILE = 256


def halves(x):
    high = x.astype(BF16)
    return high, (x - high.astype(F32)).astype(BF16)


def dot3(xs, ys, dims):
    def one(x, y):
        return lax.dot_general(x, y, (dims, ((), ())), preferred_element_type=F32)

    return one(xs[0], ys[0]) + (one(xs[0], ys[1]) + one(xs[1], ys[0]))


def sigmoid(x):
    return 1.0 / (1.0 + jnp.exp(-x))


def offsets(rows):
    starts, at = [], 0
    for r in rows:
        starts.append(at)
        at += r
    return starts


def spans(total, tile):
    return [pl.ds(start, tile) for start in range(0, total, tile)]


def wide(*shape):
    return jax.ShapeDtypeStruct(shape, F32)


def thin(*shape):
    return jax.ShapeDtypeStruct(shape, BF16)


def call(kernel, name, args, in_specs, out_shape, out_specs, flops, scratch=(), aliases=None):
    return pl.pallas_call(
        kernel,
        out_shape=out_shape,
        in_specs=in_specs,
        out_specs=out_specs,
        scratch_shapes=list(scratch),
        input_output_aliases=aliases or {},
        compiler_params=pltpu.CompilerParams(vmem_limit_bytes=VMEM_LIMIT),
        cost_estimate=pl.CostEstimate(flops=flops, bytes_accessed=4 * 1024 * 1024, transcendentals=512 * 512),
        name=name,
    )(*args)


def joined(parts, axis):
    return jnp.concatenate(parts, axis=axis)


def one_dot(x, y, dims):
    return lax.dot_general(x, y, (dims, ((), ())), preferred_element_type=F32)


def scores(xs, ys):
    (xh, xl), (yh, yl) = xs, ys
    return one_dot(joined([xh, xh, xl], 1), joined([yh, yl, yh], 1), ((1,), (1,)))


def weighted(cs, ys):
    (ch, cl), (yh, yl) = cs, ys
    return one_dot(joined([ch, ch, cl], 1), joined([yh, yl, yh], 0), ((1,), (0,)))


def coefs(xs, ys, params):
    scale, bias = params[0:1, 0:1], params[8:9, 0:1]
    return halves(scale * sigmoid(scale * scores(xs, ys) + bias))


def term(xs, ys, params):
    return weighted(coefs(xs, ys, params), ys)


LINK, CHIP = 0, 1


def by_parity(link_is_images, link_is_texts):
    even = lax.rem(lax.axis_index("dp"), 2) == 0
    pl.when(even)(link_is_images)
    pl.when(jnp.logical_not(even))(link_is_texts)


def to_output(side, source, images, texts, sem):
    first, second = (images, texts) if side == LINK else (texts, images)
    by_parity(
        pltpu.make_async_copy(source, first, sem).start,
        pltpu.make_async_copy(source, second, sem).start,
    )


def pick_kernel(parts, images, texts, *refs):
    outs, sems = refs[-1 - len(parts) : -1], refs[-1]
    for k, ((side, start, rows), out) in enumerate(zip(parts, outs)):
        span = pl.ds(start, rows)
        first, second = (images, texts) if side == LINK else (texts, images)
        by_parity(
            pltpu.make_async_copy(first.at[span], out, sems.at[k]).start,
            pltpu.make_async_copy(second.at[span], out, sems.at[k]).start,
        )
    for k, ((_, start, rows), out) in enumerate(zip(parts, outs)):
        pltpu.make_async_copy(images.at[pl.ds(start, rows)], out, sems.at[k]).wait()


def in_hbm(x):
    return pltpu.with_memory_space_constraint(x, pltpu.HBM)


def pick(images, texts, parts, *earlier):
    width = images.shape[1]
    return call(
        functools.partial(pick_kernel, parts),
        "pick",
        (in_hbm(images), in_hbm(texts), *earlier),
        [HBM] * 2 + [ANY] * len(earlier),
        [wide(rows, width) for _, _, rows in parts],
        [VMEM] * len(parts),
        0,
        [pltpu.SemaphoreType.DMA((len(parts),))],
    )


def own_kernel(scale_ref, bias_ref, chip_block, *refs):
    link_rows, (grads, high, low, params) = refs[:-4], refs[-4:]
    high[CHIP], low[CHIP] = halves(chip_block[...])
    high[LINK], low[LINK] = halves(joined([x[...] for x in link_rows], 0))
    scale, bias = scale_ref[...], bias_ref[...]
    params[0:8, :] = jnp.broadcast_to(scale, (8, 128))
    params[8:16, :] = jnp.broadcast_to(bias, (8, 128))
    ys = (high[CHIP], low[CHIP])
    for t, span in enumerate(spans(chip_block.shape[0], TILE)):
        xs = (high[LINK, span, :], low[LINK, span, :])
        logits = scale * scores(xs, ys) + bias
        shape = logits.shape
        diagonal = lax.broadcasted_iota(jnp.int32, shape, 0) + t * TILE == (
            lax.broadcasted_iota(jnp.int32, shape, 1)
        )
        sign = jnp.where(diagonal, -1.0, 1.0).astype(F32)
        coef = halves(sign * scale * sigmoid(sign * logits))
        grads[LINK, span, :] = weighted(coef, ys)
        part = dot3(coef, xs, ((0,), (0,)))
        grads[CHIP] = part if t == 0 else grads[CHIP] + part


def own(link_rows, chip_block, scale, bias):
    rows, width = chip_block.shape
    return call(
        own_kernel,
        "own_pair",
        (scale.reshape(1, 1), bias.reshape(1, 1), chip_block, *link_rows),
        [VMEM] * (3 + len(link_rows)),
        [wide(2, rows, width), thin(2, rows, width), thin(2, rows, width), wide(16, 128)],
        [VMEM] * 4,
        HINT * 18 * rows * rows * width,
    )


def both_kernel(first, params, x, yh, yl, *refs):
    before, (mate, high, low, *terms) = (None, refs) if first else (refs[0], refs[1:])
    ys = (yh[...], yl[...])
    xs = halves(x[...])
    high[...], low[...] = xs
    coef = coefs(xs, ys, params)
    start = 0
    for term_out in terms:
        rows = term_out.shape[0]
        term_out[...] = weighted([c[start : start + rows] for c in coef], ys)
        start += rows
    part = dot3(coef, xs, ((0,), (0,)))
    mate[...] = part if first else before[...] + part


def both_terms(params, x, pieces, ys, before=None):
    depth, width = x.shape
    rows = ys[0].shape[0]
    first = before is None
    inputs = (params, x, *ys) if first else (params, x, *ys, before)
    outs = [wide(rows, width), thin(depth, width), thin(depth, width)]
    outs += [wide(r, width) for r in pieces]
    return call(
        functools.partial(both_kernel, first),
        "both_terms",
        inputs,
        [VMEM] * len(inputs),
        outs,
        [VMEM] * len(outs),
        18 * rows * depth * width,
        aliases={} if first else {4: 0},
    )


def near_kernel(params, y, high, low, grads, grads_out, yh, yl):
    ys = halves(y[...])
    yh[...], yl[...] = ys
    for span in spans(y.shape[0], TILE):
        xs = (high[CHIP, span, :], low[CHIP, span, :])
        grads_out[CHIP, span, :] = grads[CHIP, span, :] + term(xs, ys, params)


def near(params, y, high, low, grads):
    rows, width = y.shape
    return call(
        near_kernel,
        "near_pair",
        (params, y, high, low, grads),
        [VMEM] * 5,
        [wide(2, rows, width)] + [thin(rows, width)] * 2,
        [VMEM] * 3,
        12 * rows * rows * width,
        aliases={4: 0},
    )


def add_kernel(side, pieces, params, *refs):
    highs, lows, (high, low, grads, grads_out) = refs[:pieces], refs[pieces : 2 * pieces], refs[2 * pieces :]
    ys = tuple(joined([y[...] for y in part], 0) if pieces > 1 else part[0][...] for part in (highs, lows))
    for span in spans(grads.shape[1], TILE):
        xs = (high[side, span, :], low[side, span, :])
        grads_out[side, span, :] = grads[side, span, :] + term(xs, ys, params)


def add_term(side, params, highs, lows, high, low, grads, hint=1):
    _, rows, width = grads.shape
    pieces = len(highs)
    last = 3 + 2 * pieces
    return call(
        functools.partial(add_kernel, side, pieces),
        "add_term",
        (params, *highs, *lows, high, low, grads),
        [VMEM] * (last + 1),
        wide(2, rows, width),
        VMEM,
        hint * 12 * rows * rows * width,
        aliases={last: 0},
    )


def finish_kernel(side, start, term_in, grads, *refs):
    images_out, texts_out, result, sem = refs[-4:]
    span = pl.ds(start, term_in.shape[0])
    result[...] = grads[side, span, :] + term_in[...]
    to_output(side, result, images_out.at[span], texts_out.at[span], sem)
    pltpu.make_async_copy(result, images_out.at[span], sem).wait()


def finish(side, start, term_in, grads, outs=()):
    _, rows, width = grads.shape
    return call(
        functools.partial(finish_kernel, side, start),
        "finish",
        (term_in, grads, *outs),
        [VMEM] * 2 + [ANY] * len(outs),
        [wide(rows, width)] * 2,
        [ANY] * 2,
        0,
        [pltpu.VMEM(term_in.shape, F32), pltpu.SemaphoreType.DMA(())],
        {2 + i: i for i in range(len(outs))},
    )


def after(value, *earlier):
    return lax.optimization_barrier((value, earlier))[0]


def body(images, texts, scale, bias):
    peers = lax.axis_size("dp")

    def over_link(x):
        return lax.ppermute(
            x, "dp", [(i, (i + 1) % peers if i % 2 else (i - 1) % peers) for i in range(peers)]
        )

    def on_chip(x):
        return lax.ppermute(x, "dp", [(i, i ^ 1) for i in range(peers)])

    rows = images.shape[0]
    head = pick(images, texts, [(LINK, 0, HEAD)])
    tail, b = pick(images, texts, [(LINK, HEAD, rows - HEAD), (CHIP, 0, rows)], *head)
    a = [*head, tail]
    a1 = [over_link(x) for x in a]
    b1 = on_chip(b)
    grads, high, low, params = own(a, b, scale, bias)
    grads, *ys = near(params, after(b1, grads), high, low, grads)
    mate, ah, al, *terms = both_terms(params, after(a1[0], grads), HEAD_TERMS, ys)
    returned = [over_link(x) for x in terms]
    mate, th, tl, *terms = both_terms(params, after(a1[1], mate), TAIL_TERMS, ys, mate)
    returned += [over_link(x) for x in terms]
    mate = on_chip(mate)
    grads = add_term(LINK, params, [after(ah, returned[0]), th], [al, tl], high, low, grads, HINT)
    outs = finish(CHIP, 0, after(mate, grads), grads)
    start = 0
    for piece in returned:
        outs = finish(LINK, start, after(piece, outs), grads, outs)
        start += piece.shape[0]
    return tuple(outs)


def solution(mesh):
    in_specs = (P("dp", None), P("dp", None), P(), P())
    out_specs = (P("dp", None), P("dp", None))
    return jax.shard_map(body, mesh=mesh, in_specs=in_specs, out_specs=out_specs, check_vma=False)
```

```python
import functools

import jax
import jax.numpy as jnp
from jax import lax
from jax.experimental import pallas as pl
from jax.experimental.pallas import tpu as pltpu
from jax.sharding import PartitionSpec as P

F32 = jnp.float32
BF16 = jnp.bfloat16
ANY = pl.BlockSpec(memory_space=pl.ANY)
HBM = pl.BlockSpec(memory_space=pltpu.HBM)
VMEM = pl.BlockSpec(memory_space=pltpu.VMEM)
VMEM_LIMIT = 20 * 1024 * 1024

HINT = 10

HEAD = 256
HEAD_TERMS = (256,)
TAIL_TERMS = (256,)
TILE = 256


def halves(x):
    high = x.astype(BF16)
    return high, (x - high.astype(F32)).astype(BF16)


def dot3(xs, ys, dims):
    def one(x, y):
        return lax.dot_general(x, y, (dims, ((), ())), preferred_element_type=F32)

    return one(xs[0], ys[0]) + (one(xs[0], ys[1]) + one(xs[1], ys[0]))


def sigmoid(x):
    return 1.0 / (1.0 + jnp.exp(-x))


def offsets(rows):
    starts, at = [], 0
    for r in rows:
        starts.append(at)
        at += r
    return starts


def spans(total, tile):
    return [pl.ds(start, tile) for start in range(0, total, tile)]


def wide(*shape):
    return jax.ShapeDtypeStruct(shape, F32)


def thin(*shape):
    return jax.ShapeDtypeStruct(shape, BF16)


def call(kernel, name, args, in_specs, out_shape, out_specs, flops, scratch=(), aliases=None):
    return pl.pallas_call(
        kernel,
        out_shape=out_shape,
        in_specs=in_specs,
        out_specs=out_specs,
        scratch_shapes=list(scratch),
        input_output_aliases=aliases or {},
        compiler_params=pltpu.CompilerParams(vmem_limit_bytes=VMEM_LIMIT),
        cost_estimate=pl.CostEstimate(flops=flops, bytes_accessed=4 * 1024 * 1024, transcendentals=512 * 512),
        name=name,
    )(*args)


def joined(parts, axis):
    return jnp.concatenate(parts, axis=axis)


def one_dot(x, y, dims):
    return lax.dot_general(x, y, (dims, ((), ())), preferred_element_type=F32)


def scores(xs, ys):
    (xh, xl), (yh, yl) = xs, ys
    return one_dot(joined([xh, xh, xl], 1), joined([yh, yl, yh], 1), ((1,), (1,)))


def weighted(cs, ys):
    (ch, cl), (yh, yl) = cs, ys
    return one_dot(joined([ch, ch, cl], 1), joined([yh, yl, yh], 0), ((1,), (0,)))


def coefs(xs, ys, params):
    scale, bias = params[0:1, 0:1], params[8:9, 0:1]
    return halves(scale * sigmoid(scale * scores(xs, ys) + bias))


def term(xs, ys, params):
    return weighted(coefs(xs, ys, params), ys)


LINK, CHIP = 0, 1


def by_parity(link_is_images, link_is_texts):
    even = lax.rem(lax.axis_index("dp"), 2) == 0
    pl.when(even)(link_is_images)
    pl.when(jnp.logical_not(even))(link_is_texts)


def to_output(side, source, images, texts, sem):
    first, second = (images, texts) if side == LINK else (texts, images)
    by_parity(
        pltpu.make_async_copy(source, first, sem).start,
        pltpu.make_async_copy(source, second, sem).start,
    )


def pick_kernel(parts, images, texts, *refs):
    outs, sems = refs[-1 - len(parts) : -1], refs[-1]
    for k, ((side, start, rows), out) in enumerate(zip(parts, outs)):
        span = pl.ds(start, rows)
        first, second = (images, texts) if side == LINK else (texts, images)
        by_parity(
            pltpu.make_async_copy(first.at[span], out, sems.at[k]).start,
            pltpu.make_async_copy(second.at[span], out, sems.at[k]).start,
        )
    for k, ((_, start, rows), out) in enumerate(zip(parts, outs)):
        pltpu.make_async_copy(images.at[pl.ds(start, rows)], out, sems.at[k]).wait()


def in_hbm(x):
    return pltpu.with_memory_space_constraint(x, pltpu.HBM)


def pick(images, texts, parts, *earlier):
    width = images.shape[1]
    return call(
        functools.partial(pick_kernel, parts),
        "pick",
        (in_hbm(images), in_hbm(texts), *earlier),
        [HBM] * 2 + [ANY] * len(earlier),
        [wide(rows, width) for _, _, rows in parts],
        [VMEM] * len(parts),
        0,
        [pltpu.SemaphoreType.DMA((len(parts),))],
    )


def own_kernel(scale_ref, bias_ref, chip_block, *refs):
    link_rows, (grads, high, low, params) = refs[:-4], refs[-4:]
    high[CHIP], low[CHIP] = halves(chip_block[...])
    high[LINK], low[LINK] = halves(joined([x[...] for x in link_rows], 0))
    scale, bias = scale_ref[...], bias_ref[...]
    params[0:8, :] = jnp.broadcast_to(scale, (8, 128))
    params[8:16, :] = jnp.broadcast_to(bias, (8, 128))
    ys = (high[CHIP], low[CHIP])
    for t, span in enumerate(spans(chip_block.shape[0], TILE)):
        xs = (high[LINK, span, :], low[LINK, span, :])
        logits = scale * scores(xs, ys) + bias
        shape = logits.shape
        diagonal = lax.broadcasted_iota(jnp.int32, shape, 0) + t * TILE == (
            lax.broadcasted_iota(jnp.int32, shape, 1)
        )
        sign = jnp.where(diagonal, -1.0, 1.0).astype(F32)
        coef = halves(sign * scale * sigmoid(sign * logits))
        grads[LINK, span, :] = weighted(coef, ys)
        part = dot3(coef, xs, ((0,), (0,)))
        grads[CHIP] = part if t == 0 else grads[CHIP] + part


def own(link_rows, chip_block, scale, bias):
    rows, width = chip_block.shape
    return call(
        own_kernel,
        "own_pair",
        (scale.reshape(1, 1), bias.reshape(1, 1), chip_block, *link_rows),
        [VMEM] * (3 + len(link_rows)),
        [wide(2, rows, width), thin(2, rows, width), thin(2, rows, width), wide(16, 128)],
        [VMEM] * 4,
        HINT * 18 * rows * rows * width,
    )


def both_kernel(first, params, x, yh, yl, *refs):
    before, (mate, high, low, *terms) = (None, refs) if first else (refs[0], refs[1:])
    ys = (yh[...], yl[...])
    xs = halves(x[...])
    high[...], low[...] = xs
    coef = coefs(xs, ys, params)
    start = 0
    for term_out in terms:
        rows = term_out.shape[0]
        term_out[...] = weighted([c[start : start + rows] for c in coef], ys)
        start += rows
    part = dot3(coef, xs, ((0,), (0,)))
    mate[...] = part if first else before[...] + part


def both_terms(params, x, pieces, ys, before=None):
    depth, width = x.shape
    rows = ys[0].shape[0]
    first = before is None
    inputs = (params, x, *ys) if first else (params, x, *ys, before)
    outs = [wide(rows, width), thin(depth, width), thin(depth, width)]
    outs += [wide(r, width) for r in pieces]
    return call(
        functools.partial(both_kernel, first),
        "both_terms",
        inputs,
        [VMEM] * len(inputs),
        outs,
        [VMEM] * len(outs),
        18 * rows * depth * width,
        aliases={} if first else {4: 0},
    )


def near_kernel(params, y, high, low, grads, grads_out, yh, yl):
    ys = halves(y[...])
    yh[...], yl[...] = ys
    for span in spans(y.shape[0], TILE)[:1]:
        xs = (high[CHIP, span, :], low[CHIP, span, :])
        grads_out[CHIP, span, :] = grads[CHIP, span, :] + term(xs, ys, params)


def near(params, y, high, low, grads):
    rows, width = y.shape
    return call(
        near_kernel,
        "near_pair",
        (params, y, high, low, grads),
        [VMEM] * 5,
        [wide(2, rows, width)] + [thin(rows, width)] * 2,
        [VMEM] * 3,
        12 * rows * rows * width,
        aliases={4: 0},
    )


def add_kernel(side, pieces, skip, params, *refs):
    highs, lows, (high, low, grads, grads_out) = refs[:pieces], refs[pieces : 2 * pieces], refs[2 * pieces :]
    ys = tuple(joined([y[...] for y in part], 0) if pieces > 1 else part[0][...] for part in (highs, lows))
    for span in spans(grads.shape[1], TILE)[skip:]:
        xs = (high[side, span, :], low[side, span, :])
        grads_out[side, span, :] = grads[side, span, :] + term(xs, ys, params)


def add_term(side, params, highs, lows, high, low, grads, hint=1, skip=0):
    _, rows, width = grads.shape
    pieces = len(highs)
    last = 3 + 2 * pieces
    return call(
        functools.partial(add_kernel, side, pieces, skip),
        "add_term",
        (params, *highs, *lows, high, low, grads),
        [VMEM] * (last + 1),
        wide(2, rows, width),
        VMEM,
        hint * 12 * rows * rows * width,
        aliases={last: 0},
    )


def finish_kernel(side, start, term_in, grads, *refs):
    images_out, texts_out, result, sem = refs[-4:]
    span = pl.ds(start, term_in.shape[0])
    result[...] = grads[side, span, :] + term_in[...]
    to_output(side, result, images_out.at[span], texts_out.at[span], sem)
    pltpu.make_async_copy(result, images_out.at[span], sem).wait()


def finish(side, start, term_in, grads, outs=()):
    _, rows, width = grads.shape
    return call(
        functools.partial(finish_kernel, side, start),
        "finish",
        (term_in, grads, *outs),
        [VMEM] * 2 + [ANY] * len(outs),
        [wide(rows, width)] * 2,
        [ANY] * 2,
        0,
        [pltpu.VMEM(term_in.shape, F32), pltpu.SemaphoreType.DMA(())],
        {2 + i: i for i in range(len(outs))},
    )


def after(value, *earlier):
    return lax.optimization_barrier((value, earlier))[0]


def body(images, texts, scale, bias):
    peers = lax.axis_size("dp")

    def over_link(x):
        return lax.ppermute(
            x, "dp", [(i, (i + 1) % peers if i % 2 else (i - 1) % peers) for i in range(peers)]
        )

    def on_chip(x):
        return lax.ppermute(x, "dp", [(i, i ^ 1) for i in range(peers)])

    rows = images.shape[0]
    head = pick(images, texts, [(LINK, 0, HEAD)])
    tail, b = pick(images, texts, [(LINK, HEAD, rows - HEAD), (CHIP, 0, rows)], *head)
    a = [*head, tail]
    a1 = [over_link(x) for x in a]
    b1 = on_chip(b)
    grads, high, low, params = own(a, b, scale, bias)
    grads, *ys = near(params, after(b1, grads), high, low, grads)
    mate, ah, al, *terms = both_terms(params, after(a1[0], grads), HEAD_TERMS, ys)
    returned = [over_link(x) for x in terms]
    grads = add_term(CHIP, params, *([after(y, mate)] for y in ys), high, low, grads, skip=1)
    mate, th, tl, *terms = both_terms(params, after(a1[1], grads), TAIL_TERMS, ys, mate)
    returned += [over_link(x) for x in terms]
    mate = on_chip(mate)
    grads = add_term(LINK, params, [after(ah, returned[0]), th], [al, tl], high, low, grads, HINT)
    outs = finish(CHIP, 0, after(mate, grads), grads)
    start = 0
    for piece in returned:
        outs = finish(LINK, start, after(piece, outs), grads, outs)
        start += piece.shape[0]
    return tuple(outs)


def solution(mesh):
    in_specs = (P("dp", None), P("dp", None), P(), P())
    out_specs = (P("dp", None), P("dp", None))
    return jax.shard_map(body, mesh=mesh, in_specs=in_specs, out_specs=out_specs, check_vma=False)
```
